512 devices in a mesh: gauss: 128 (over x, z, core), img: 4 (over y).
Axes of the slice: x: 4, y: 4, z: 16, core: 2. Of those that a mesh axis runs over, the one named last changes fastest.
Arguments:
- params: float32 [59, 524288], P(None, 'gauss'), as said below
- cameras: float32 [4, 16], P('img'), as said below
- send_rows: int32 [4, 65536], P('img', 'gauss'), may hold values from 0 to 4095
- tile_ids: int32 [4, 256], P('img', 'gauss'), may hold values from 0 to 255, as said below
- lists: int32 [4, 256, 256], P('img', 'gauss'), may hold values from 0 to 511, as said below
- counts: int32 [4, 256], P('img', 'gauss'), may hold values from 1 to 256, as said below
- targets: float32 [4, 256, 3, 256], P('img', 'gauss'), may hold values from -3 to 4
Outputs:
- grads: float32 [59, 524288], P(None, ('gauss', 'img'))
- rendered: float32 [4, 256, 3, 256], P('img', 'gauss')
The draws below stay inside these ranges and needn't reach their ends.
Inputs may be any that keep to these rules, and one draw needn't show every extreme that they name: `params`: means at depth 3 to 5 in front of every view; log scales within -4.5 and -3.2, quaternion with w in [1, 2] and x, y, z in [-1, 1], opacity logits within -4 and -1, coefficients of order one. `cameras`: rotation by angles of at most 0.006 about each axis, translation entries within 0.02, focal lengths 255 to 257, centre at the middle of the image of 16 x 16 tiles, at pixel (128, 128). `tile_ids`: a permutation of the view's tiles; the 2 tiles of one owner form one of 128 groups of tiles that are the same in every view. `lists`: row s * 4 + k of a tile owner's received rows comes from Gaussian owner s; of every sender's 4 rows, each run of 2 belongs to one of the owner's tiles, a list names only rows of its own tile's runs, and its valid entries are distinct. `counts`: a tile has the same count in every view; in every view all tiles of one owner have the most, and another tile has 1.
All inputs are finite; a program needn't handle non-finite values.
Results may differ from the reference program's by a relative error of at most 0.0045.
Values sent between devices are 32-bit elements; how exact they have to be, the bound alone decides.
A program may use at most 64 MiB of HBM per device.

```python
import jax
import jax.numpy as jnp
from jax import lax

FEATS = 9
TILE_PIX = 256
TILES_X = 16
G_DEV = 4096
PER_TILE = 2
SLOTS = 2
CAP = 4
LIST = 256
BLOCK = 256
GAUSS = 524288
TILES = 256
IMAGES = 4
ROUTES = 65536
N_GAUSS = 128


sh_zero = 0.28209479177387814


sh_one = 0.4886025119029199


sh_two = [1.0925484305920792, -1.0925484305920792, 0.31539156525252005, -1.0925484305920792, 0.5462742152960396]


sh_three = [-0.5900435899266435, 2.890611442640554, -0.4570457994644658, 0.3731763325901154, -0.4570457994644658, 1.445305721320277, -0.5900435899266435]


def sum_terms_drawn(basis, coeffs):
    accum = basis[0][None, :] * coeffs[0]
    for k in range(1, 16):
        accum = accum + basis[k][None, :] * coeffs[k]
    return accum


def project_drawn(rows, camera):
    world = [rows[0], rows[1], rows[2]]
    rotation = [[camera[3 * i + j] for j in range(3)] for i in range(3)]
    shift = [camera[9], camera[10], camera[11]]
    focal_x, focal_y, centre_x, centre_y = (camera[12], camera[13], camera[14], camera[15])
    in_camera = [rotation[i][0] * world[0] + rotation[i][1] * world[1] + rotation[i][2] * world[2] + shift[i] for i in range(3)]
    depth = in_camera[2]
    pos_u = focal_x * in_camera[0] / depth + centre_x
    pos_v = focal_y * in_camera[1] / depth + centre_y
    zero_row = jnp.zeros_like(depth)
    jacobian = [[focal_x / depth, zero_row, -focal_x * in_camera[0] / (depth * depth)], [zero_row, focal_y / depth, -focal_y * in_camera[1] / (depth * depth)]]
    quat = rows[6:10]
    qnorm = jnp.sqrt(jnp.sum(quat * quat, axis=0))
    q_w, q_x, q_y, q_z = (quat[0] / qnorm, quat[1] / qnorm, quat[2] / qnorm, quat[3] / qnorm)
    rot_gauss = [[1.0 - 2.0 * (q_y * q_y + q_z * q_z), 2.0 * (q_x * q_y - q_w * q_z), 2.0 * (q_x * q_z + q_w * q_y)], [2.0 * (q_x * q_y + q_w * q_z), 1.0 - 2.0 * (q_x * q_x + q_z * q_z), 2.0 * (q_y * q_z - q_w * q_x)], [2.0 * (q_x * q_z - q_w * q_y), 2.0 * (q_y * q_z + q_w * q_x), 1.0 - 2.0 * (q_x * q_x + q_y * q_y)]]
    scales = jnp.exp(rows[3:6])
    screen_map = [[jacobian[a][0] * rotation[0][j] + jacobian[a][1] * rotation[1][j] + jacobian[a][2] * rotation[2][j] for j in range(3)] for a in range(2)]
    spread = [[(screen_map[a][0] * rot_gauss[0][k] + screen_map[a][1] * rot_gauss[1][k] + screen_map[a][2] * rot_gauss[2][k]) * scales[k] for k in range(3)] for a in range(2)]
    cov_xx = spread[0][0] * spread[0][0] + spread[0][1] * spread[0][1] + spread[0][2] * spread[0][2] + 0.3
    cov_xy = spread[0][0] * spread[1][0] + spread[0][1] * spread[1][1] + spread[0][2] * spread[1][2]
    cov_yy = spread[1][0] * spread[1][0] + spread[1][1] * spread[1][1] + spread[1][2] * spread[1][2] + 0.3
    determ = cov_xx * cov_yy - cov_xy * cov_xy
    opacity = jax.nn.sigmoid(rows[10])
    centre = [-(rotation[0][j] * shift[0] + rotation[1][j] * shift[1] + rotation[2][j] * shift[2]) for j in range(3)]
    view = [world[j] - centre[j] for j in range(3)]
    length = jnp.sqrt(view[0] * view[0] + view[1] * view[1] + view[2] * view[2])
    dir_x, dir_y, dir_z = (view[0] / length, view[1] / length, view[2] / length)
    sq_x, sq_y, sq_z = (dir_x * dir_x, dir_y * dir_y, dir_z * dir_z)
    basis = [sh_zero + zero_row, -sh_one * dir_y, sh_one * dir_z, -sh_one * dir_x, sh_two[0] * dir_x * dir_y, sh_two[1] * dir_y * dir_z, sh_two[2] * (2.0 * sq_z - sq_x - sq_y), sh_two[3] * dir_x * dir_z, sh_two[4] * (sq_x - sq_y), sh_three[0] * dir_y * (3.0 * sq_x - sq_y), sh_three[1] * dir_x * dir_y * dir_z, sh_three[2] * dir_y * (4.0 * sq_z - sq_x - sq_y), sh_three[3] * dir_z * (2.0 * sq_z - 3.0 * sq_x - 3.0 * sq_y), sh_three[4] * dir_x * (4.0 * sq_z - sq_x - sq_y), sh_three[5] * dir_z * (sq_x - sq_y), sh_three[6] * dir_x * (sq_x - 3.0 * sq_y)]
    coeffs = rows[11:].reshape(16, 3, rows.shape[1])
    colour = 0.5 + sum_terms_drawn(basis, coeffs)
    return jnp.stack([pos_u, pos_v, cov_yy / determ, -cov_xy / determ, cov_xx / determ, colour[0], colour[1], colour[2], opacity])


def advance_drawn(carry, block_rows, start, pixel_x, pixel_y, count_now, strict_upper):
    log_trans, colour = carry
    width = block_rows.shape[1]
    off_x = block_rows[0][None, :] - pixel_x[:, None]
    off_y = block_rows[1][None, :] - pixel_y[:, None]
    quad = block_rows[2] * off_x * off_x + 2.0 * block_rows[3] * off_x * off_y + block_rows[4] * off_y * off_y
    live = (start + jnp.arange(width, dtype=jnp.int32) < count_now).astype(jnp.float32)
    alpha = live[None, :] * block_rows[8][None, :] * jnp.exp(-0.5 * quad)
    log_keep = jnp.log1p(-alpha)
    before = jnp.dot(log_keep, strict_upper, precision=lax.Precision.HIGHEST)
    weight = alpha * jnp.exp(log_trans[:, None] + before)
    colour = colour + jnp.dot(block_rows[5:8], weight.T, precision=lax.Precision.HIGHEST)
    return (log_trans + jnp.sum(log_keep, axis=1), colour)


def render_drawn(rows, tile, count_now):
    pixel = jnp.arange(TILE_PIX, dtype=jnp.int32)
    pixel_x = (tile % TILES_X * 16 + pixel % 16).astype(jnp.float32)
    pixel_y = (tile // TILES_X * 16 + pixel // 16).astype(jnp.float32)
    nblocks = rows.shape[1] // BLOCK
    stacked = rows.reshape(FEATS, nblocks, BLOCK).transpose(1, 0, 2)
    starts = jnp.arange(nblocks, dtype=jnp.int32) * BLOCK
    iota = jnp.arange(BLOCK, dtype=jnp.int32)
    strict_upper = (iota[:, None] < iota[None, :]).astype(jnp.float32)

    def step(carry, inputs):
        block_rows, start = inputs
        return (advance_drawn(carry, block_rows, start, pixel_x, pixel_y, count_now, strict_upper), None)
    init = (jnp.zeros((TILE_PIX,), jnp.float32), jnp.zeros((3, TILE_PIX), jnp.float32))
    final, unused = lax.scan(step, init, (stacked, starts))
    return final[1]


def tile_layout(key):
    per_tile = PER_TILE
    span_rows = N_GAUSS * per_tile
    most_live = min(LIST, span_rows)
    canonical = jax.random.permutation(jax.random.fold_in(key, 101), TILES).astype(jnp.int32)
    factor_one = jax.random.randint(jax.random.fold_in(key, 102), (TILES,), 1, most_live + 1)
    factor_two = jax.random.randint(jax.random.fold_in(key, 103), (TILES,), max(1, most_live // 4), most_live + 1)
    tile_loads = (factor_one * factor_two + most_live - 1) // most_live
    position = jnp.arange(TILES, dtype=jnp.int32)
    tile_loads = jnp.where(position < SLOTS, most_live, tile_loads)
    tile_loads = jnp.where(position == SLOTS, 1, tile_loads).astype(jnp.int32)
    entry_order = jax.vmap(lambda subkey: jax.random.permutation(subkey, span_rows))(jax.random.split(jax.random.fold_in(key, 104), TILES)).astype(jnp.int32)
    gauss_order = jax.vmap(lambda subkey: jax.random.permutation(subkey, G_DEV))(jax.random.split(jax.random.fold_in(key, 105), N_GAUSS)).astype(jnp.int32)
    group_order = jax.vmap(lambda subkey: jax.random.permutation(subkey, N_GAUSS))(jax.random.split(jax.random.fold_in(key, 106), IMAGES)).astype(jnp.int32)
    slot_order = jax.vmap(lambda subkey: jax.random.permutation(subkey, SLOTS))(jax.random.split(jax.random.fold_in(key, 107), IMAGES * N_GAUSS)).astype(jnp.int32)
    slot_order = slot_order.reshape(IMAGES, N_GAUSS, SLOTS)
    return (canonical, tile_loads, entry_order, gauss_order, group_order, slot_order)


def held_positions(layout):
    return layout[4][:, :, None] * SLOTS + layout[5]


def draw_params(key, part):
    layout = tile_layout(key)
    key = jax.random.fold_in(key, 11)
    keys = jax.random.split(key, 12)
    per_tile = PER_TILE
    span_rows = N_GAUSS * per_tile
    source = jnp.arange(N_GAUSS, dtype=jnp.int32)
    inverse_gauss = jnp.zeros((N_GAUSS, G_DEV), jnp.int32).at[source[:, None], layout[3]].set(jnp.arange(G_DEV, dtype=jnp.int32)[None, :])
    homed = inverse_gauss < N_GAUSS * CAP
    position = jnp.minimum(inverse_gauss // per_tile, TILES - 1)
    level = inverse_gauss % per_tile
    inverse_entry = jnp.zeros((TILES, span_rows), jnp.int32).at[jnp.arange(TILES, dtype=jnp.int32)[:, None], layout[2]].set(jnp.arange(span_rows, dtype=jnp.int32)[None, :])
    code = source[:, None] + N_GAUSS * level
    depth_rank = inverse_entry[position, code]
    listed = homed & (depth_rank < layout[1][position])
    tile = layout[0][position]
    width_px = 16.0 * TILES_X
    height_px = 16.0 * (TILES // TILES_X)
    shape = (N_GAUSS, G_DEV)
    jitter_x = jax.random.uniform(keys[0], shape, jnp.float32, -7.5, 7.5)
    jitter_y = jax.random.uniform(keys[1], shape, jnp.float32, -7.5, 7.5)
    loose_x = jax.random.uniform(keys[2], shape, jnp.float32, 0.0, width_px)
    loose_y = jax.random.uniform(keys[3], shape, jnp.float32, 0.0, height_px)
    home_x = (16 * (tile % TILES_X)).astype(jnp.float32) + 7.5 + jitter_x
    home_y = (16 * (tile // TILES_X)).astype(jnp.float32) + 7.5 + jitter_y
    pixel_x = jnp.where(homed, home_x, loose_x)
    pixel_y = jnp.where(homed, home_y, loose_y)
    loose_depth = jax.random.uniform(keys[4], shape, jnp.float32, 3.0, 5.0)
    depth_step = jax.random.uniform(keys[5], shape, jnp.float32, 0.1, 0.9)
    ranked_depth = 3.0 + 2.0 * (depth_rank.astype(jnp.float32) + depth_step) / LIST
    depth = jnp.where(listed, ranked_depth, loose_depth)
    world_x = (pixel_x - 0.5 * width_px) * depth / 256.0
    world_y = (pixel_y - 0.5 * height_px) * depth / 256.0
    log_scale = jax.random.uniform(keys[6], (3, GAUSS), jnp.float32, -4.5, -3.2)
    quat_w = jax.random.uniform(keys[7], (1, GAUSS), jnp.float32, 1.0, 2.0)
    quat_v = jax.random.uniform(keys[8], (3, GAUSS), jnp.float32, -1.0, 1.0)
    logit = jax.random.uniform(keys[9], (1, GAUSS), jnp.float32, -4.0, -1.0)
    coeffs = 0.3 * jax.random.normal(keys[10], (16, 3, GAUSS), jnp.float32)
    coeffs = coeffs.at[0].multiply(2.7)
    return jnp.concatenate([world_x.reshape(1, GAUSS), world_y.reshape(1, GAUSS), depth.reshape(1, GAUSS), log_scale, quat_w, quat_v, logit, coeffs.reshape(48, GAUSS)], axis=0)


def draw_cameras(key, part):
    key = jax.random.fold_in(key, 12)
    keys = jax.random.split(key, 3)
    angles = jax.random.uniform(keys[0], (3, IMAGES), jnp.float32, -0.006, 0.006)
    shift = jax.random.uniform(keys[1], (3, IMAGES), jnp.float32, -0.02, 0.02)
    focal = jax.random.uniform(keys[2], (2, IMAGES), jnp.float32, 255.0, 257.0)
    cos_a, sin_a = (jnp.cos(angles[0]), jnp.sin(angles[0]))
    cos_b, sin_b = (jnp.cos(angles[1]), jnp.sin(angles[1]))
    cos_c, sin_c = (jnp.cos(angles[2]), jnp.sin(angles[2]))
    entries = [cos_b * cos_c, sin_a * sin_b * cos_c - cos_a * sin_c, cos_a * sin_b * cos_c + sin_a * sin_c, cos_b * sin_c, sin_a * sin_b * sin_c + cos_a * cos_c, cos_a * sin_b * sin_c - sin_a * cos_c, -sin_b, sin_a * cos_b, cos_a * cos_b, shift[0], shift[1], shift[2], focal[0], focal[1], jnp.zeros((IMAGES,), jnp.float32) + 8.0 * TILES_X, jnp.zeros((IMAGES,), jnp.float32) + 8.0 * (TILES // TILES_X)]
    return jnp.stack(entries, axis=1)


def draw_send_rows(key, part):
    layout = tile_layout(key)
    key = jax.random.fold_in(key, 21)
    picked = layout[4][:, :, None] * CAP + jnp.arange(CAP, dtype=jnp.int32)[None, None, :]
    source = jnp.arange(N_GAUSS, dtype=jnp.int32)
    values = layout[3][source[None, :, None, None], picked[:, None, :, :]]
    return values.reshape(IMAGES, ROUTES).astype(jnp.int32)


def draw_tile_ids(key, part):
    layout = tile_layout(key)
    key = jax.random.fold_in(key, 22)
    return layout[0][held_positions(layout)].reshape(IMAGES, TILES).astype(jnp.int32)


def draw_counts(key, part):
    layout = tile_layout(key)
    key = jax.random.fold_in(key, 13)
    return layout[1][held_positions(layout)].reshape(IMAGES, TILES).astype(jnp.int32)


def draw_lists(key, part):
    layout = tile_layout(key)
    key = jax.random.fold_in(key, 23)
    keys = jax.random.split(key, 2)
    per_tile = PER_TILE
    span_rows = N_GAUSS * per_tile
    held = held_positions(layout)
    entry = jnp.minimum(jnp.arange(LIST, dtype=jnp.int32), span_rows - 1)
    chosen = layout[2][held[..., None], entry[None, None, None, :]]
    live = jnp.arange(LIST, dtype=jnp.int32)[None, None, None, :] < layout[1][held][..., None]
    shape = (IMAGES, N_GAUSS, SLOTS, LIST)
    pad_source = jax.random.randint(keys[0], shape, 0, N_GAUSS)
    pad_level = jax.random.randint(keys[1], shape, 0, per_tile)
    source = jnp.where(live, chosen % N_GAUSS, pad_source)
    level = jnp.where(live, chosen // N_GAUSS, pad_level)
    rows = source * CAP + layout[5][..., None] * per_tile + level
    return rows.reshape(IMAGES, TILES, LIST).astype(jnp.int32)


def draw_targets(key, part):
    params = draw_params(key, part)
    cameras = draw_cameras(key, part)
    send_rows = draw_send_rows(key, part)
    tile_ids = draw_tile_ids(key, part)
    lists = draw_lists(key, part)
    counts = draw_counts(key, part)
    key = jax.random.fold_in(key, 31)
    images = []
    for image in range(IMAGES):
        routes = send_rows[image].reshape(N_GAUSS, N_GAUSS, CAP)
        global_ids = routes + (jnp.arange(N_GAUSS, dtype=jnp.int32) * G_DEV)[:, None, None]
        by_owner = global_ids.transpose(1, 0, 2).reshape(N_GAUSS, N_GAUSS * CAP)
        owner = jnp.arange(TILES, dtype=jnp.int32) // SLOTS
        names = by_owner[owner[:, None], lists[image]]
        features = project_drawn(params, cameras[image])

        def per_slot(inputs):
            entries, count_now, tile = inputs
            return render_drawn(jnp.take(features, entries, axis=1), tile, count_now)
        images.append(lax.map(per_slot, (names, counts[image], tile_ids[image])))
    shown = jnp.stack(images)
    noise = jax.random.uniform(key, shown.shape, jnp.float32, -0.005, 0.005)
    return (shown + noise).astype(jnp.float32)


def setup_inputs(seed: int = 0) -> dict:
    arg_keys = jax.random.split(jax.random.key(seed), 8)
    return {
        "params": draw_params(jax.random.fold_in(arg_keys[7], 71), 0),
        "cameras": draw_cameras(jax.random.fold_in(arg_keys[7], 71), 0),
        "send_rows": draw_send_rows(jax.random.fold_in(arg_keys[7], 71), 0),
        "tile_ids": draw_tile_ids(jax.random.fold_in(arg_keys[7], 71), 0),
        "lists": draw_lists(jax.random.fold_in(arg_keys[7], 71), 0),
        "counts": draw_counts(jax.random.fold_in(arg_keys[7], 71), 0),
        "targets": draw_targets(jax.random.fold_in(arg_keys[7], 71), 0),
    }


sh_zero = 0.28209479177387814
sh_one = 0.4886025119029199
sh_two = [1.0925484305920792, -1.0925484305920792, 0.31539156525252005, -1.0925484305920792, 0.5462742152960396]
sh_three = [-0.5900435899266435, 2.890611442640554, -0.4570457994644658, 0.3731763325901154, -0.4570457994644658, 1.445305721320277, -0.5900435899266435]

def project(rows, camera):
    world = [rows[0], rows[1], rows[2]]
    rotation = [[camera[3 * i + j] for j in range(3)] for i in range(3)]
    shift = [camera[9], camera[10], camera[11]]
    focal_x, focal_y, centre_x, centre_y = (camera[12], camera[13], camera[14], camera[15])
    in_camera = [rotation[i][0] * world[0] + rotation[i][1] * world[1] + rotation[i][2] * world[2] + shift[i] for i in range(3)]
    depth = in_camera[2]
    pos_u = focal_x * in_camera[0] / depth + centre_x
    pos_v = focal_y * in_camera[1] / depth + centre_y
    zero_row = jnp.zeros_like(depth)
    jacobian = [[focal_x / depth, zero_row, -focal_x * in_camera[0] / (depth * depth)], [zero_row, focal_y / depth, -focal_y * in_camera[1] / (depth * depth)]]
    quat = rows[6:10]
    qnorm = jnp.sqrt(lax.optimization_barrier(jnp.sum(quat * quat, axis=0)))
    q_w, q_x, q_y, q_z = (quat[0] / qnorm, quat[1] / qnorm, quat[2] / qnorm, quat[3] / qnorm)
    rot_gauss = [[1.0 - 2.0 * (q_y * q_y + q_z * q_z), 2.0 * (q_x * q_y - q_w * q_z), 2.0 * (q_x * q_z + q_w * q_y)], [2.0 * (q_x * q_y + q_w * q_z), 1.0 - 2.0 * (q_x * q_x + q_z * q_z), 2.0 * (q_y * q_z - q_w * q_x)], [2.0 * (q_x * q_z - q_w * q_y), 2.0 * (q_y * q_z + q_w * q_x), 1.0 - 2.0 * (q_x * q_x + q_y * q_y)]]
    scales = jnp.exp(rows[3:6])
    screen_map = [[jacobian[a][0] * rotation[0][j] + jacobian[a][1] * rotation[1][j] + jacobian[a][2] * rotation[2][j] for j in range(3)] for a in range(2)]
    spread = [[(screen_map[a][0] * rot_gauss[0][k] + screen_map[a][1] * rot_gauss[1][k] + screen_map[a][2] * rot_gauss[2][k]) * scales[k] for k in range(3)] for a in range(2)]
    cov_xx = spread[0][0] * spread[0][0] + spread[0][1] * spread[0][1] + spread[0][2] * spread[0][2] + 0.3
    cov_xy = spread[0][0] * spread[1][0] + spread[0][1] * spread[1][1] + spread[0][2] * spread[1][2]
    cov_yy = spread[1][0] * spread[1][0] + spread[1][1] * spread[1][1] + spread[1][2] * spread[1][2] + 0.3
    determ = cov_xx * cov_yy - cov_xy * cov_xy
    opacity = jax.nn.sigmoid(rows[10])
    centre = [-(rotation[0][j] * shift[0] + rotation[1][j] * shift[1] + rotation[2][j] * shift[2]) for j in range(3)]
    view = [world[j] - centre[j] for j in range(3)]
    length = jnp.sqrt(view[0] * view[0] + view[1] * view[1] + view[2] * view[2])
    dir_x, dir_y, dir_z = (view[0] / length, view[1] / length, view[2] / length)
    sq_x, sq_y, sq_z = (dir_x * dir_x, dir_y * dir_y, dir_z * dir_z)
    basis = [sh_zero + zero_row, -sh_one * dir_y, sh_one * dir_z, -sh_one * dir_x, sh_two[0] * dir_x * dir_y, sh_two[1] * dir_y * dir_z, sh_two[2] * (2.0 * sq_z - sq_x - sq_y), sh_two[3] * dir_x * dir_z, sh_two[4] * (sq_x - sq_y), sh_three[0] * dir_y * (3.0 * sq_x - sq_y), sh_three[1] * dir_x * dir_y * dir_z, sh_three[2] * dir_y * (4.0 * sq_z - sq_x - sq_y), sh_three[3] * dir_z * (2.0 * sq_z - 3.0 * sq_x - 3.0 * sq_y), sh_three[4] * dir_x * (4.0 * sq_z - sq_x - sq_y), sh_three[5] * dir_z * (sq_x - sq_y), sh_three[6] * dir_x * (sq_x - 3.0 * sq_y)]
    coeffs = rows[11:].reshape(16, 3, rows.shape[1])
    colour = 0.5 + sum_terms(basis, coeffs)
    return jnp.stack([pos_u, pos_v, cov_yy / determ, -cov_xy / determ, cov_xx / determ, colour[0], colour[1], colour[2], opacity])

def sum_terms(basis, coeffs):
    accum = basis[0][None, :] * coeffs[0]
    for k in range(1, 16):
        accum = accum + basis[k][None, :] * coeffs[k]
    return accum

def advance(carry, block_rows, start, pixel_x, pixel_y, count_now, strict_upper):
    log_trans, colour = carry
    width = block_rows.shape[1]
    off_x = block_rows[0][None, :] - pixel_x[:, None]
    off_y = block_rows[1][None, :] - pixel_y[:, None]
    quad = block_rows[2] * off_x * off_x + 2.0 * block_rows[3] * off_x * off_y + block_rows[4] * off_y * off_y
    live = (start + jnp.arange(width, dtype=jnp.int32) < count_now).astype(jnp.float32)
    alpha = live[None, :] * block_rows[8][None, :] * jnp.exp(-0.5 * quad)
    log_keep = jnp.log1p(-alpha)
    before = jnp.dot(log_keep, strict_upper, precision=lax.Precision.HIGHEST)
    weight = alpha * jnp.exp(log_trans[:, None] + before)
    colour = colour + jnp.dot(block_rows[5:8], weight.T, precision=lax.Precision.HIGHEST)
    return (log_trans + lax.optimization_barrier(jnp.sum(log_keep, axis=1)), colour)

def render(rows, tile, count_now):
    pixel = jnp.arange(TILE_PIX, dtype=jnp.int32)
    pixel_x = (tile % TILES_X * 16 + pixel % 16).astype(jnp.float32)
    pixel_y = (tile // TILES_X * 16 + pixel // 16).astype(jnp.float32)
    nblocks = rows.shape[1] // BLOCK
    stacked = rows.reshape(FEATS, nblocks, BLOCK).transpose(1, 0, 2)
    starts = jnp.arange(nblocks, dtype=jnp.int32) * BLOCK
    iota = jnp.arange(BLOCK, dtype=jnp.int32)
    strict_upper = (iota[:, None] < iota[None, :]).astype(jnp.float32)

    def step(carry, inputs):
        block_rows, start = inputs
        return (advance(carry, block_rows, start, pixel_x, pixel_y, count_now, strict_upper), None)
    init = (jnp.zeros((TILE_PIX,), jnp.float32), jnp.zeros((3, TILE_PIX), jnp.float32))
    final, unused = lax.scan(step, init, (stacked, starts))
    return final[1]

def reference(params, cameras, send_rows, tile_ids, lists, counts, targets):
    grads = jnp.zeros_like(params)
    images = []
    for image in range(IMAGES):
        routes = send_rows[image].reshape(N_GAUSS, N_GAUSS, CAP)
        global_ids = routes + (jnp.arange(N_GAUSS, dtype=jnp.int32) * G_DEV)[:, None, None]
        by_owner = global_ids.transpose(1, 0, 2).reshape(N_GAUSS, N_GAUSS * CAP)
        owner = jnp.arange(TILES, dtype=jnp.int32) // SLOTS
        names = by_owner[owner[:, None], lists[image]]
        camera = cameras[image]
        features, pullback = jax.vjp(lambda rows: project(rows, camera), params)

        def per_slot(accum, inputs):
            entries, count_now, tile, target = inputs
            tile_rows = jnp.take(features, entries, axis=1)
            colour, tile_back = jax.vjp(lambda rows: render(rows, tile, count_now), tile_rows)
            grad_tile = tile_back(colour - target)[0]
            return (accum.at[:, entries].add(grad_tile), colour)
        grad_feats, colours = lax.scan(per_slot, jnp.zeros_like(features), (names, counts[image], tile_ids[image], targets[image]))
        grads = grads + pullback(grad_feats)[0]
        images.append(colours)
    return (grads, jnp.stack(images))
```

```python
import jax
import jax.numpy as jnp
from jax import lax
from jax.experimental import pallas as pl
from jax.experimental.pallas import tpu as pltpu
from jax.sharding import PartitionSpec as P

MESH = pl.DeviceIdType.MESH
F32 = jnp.float32
BF16 = jnp.bfloat16
HIGHEST = lax.Precision.HIGHEST

FEATS = 9
PARAMS = 59
G_DEV = 4096
QUARTER = 1024
ROWS = 512
LIST = 256

sh_zero = 0.28209479177387814
sh_one = 0.4886025119029199
sh_two = [1.0925484305920792, -1.0925484305920792, 0.31539156525252005, -1.0925484305920792, 0.5462742152960396]
sh_three = [
    -0.5900435899266435,
    2.890611442640554,
    -0.4570457994644658,
    0.3731763325901154,
    -0.4570457994644658,
    1.445305721320277,
    -0.5900435899266435,
]


def project_rows(rows, camera):
    m = rows[0:3]
    rot = [[camera[3 * i + j] for j in range(3)] for i in range(3)]
    shift = camera[9:12]
    focal_x, focal_y, centre_x, centre_y = camera[12:16]
    p = [rot[i][0] * m[0] + rot[i][1] * m[1] + rot[i][2] * m[2] + shift[i] for i in range(3)]
    inv_z = 1.0 / p[2]
    xn, yn = p[0] * inv_z, p[1] * inv_z
    u = focal_x * xn + centre_x
    v = focal_y * yn + centre_y
    jx, jy = focal_x * inv_z, focal_y * inv_z
    q = rows[6:10]
    inv_q = 1.0 / jnp.sqrt(q[0] * q[0] + q[1] * q[1] + q[2] * q[2] + q[3] * q[3])
    w, x, y, z = (t * inv_q for t in q)
    rg = [
        [1.0 - 2.0 * (y * y + z * z), 2.0 * (x * y - w * z), 2.0 * (x * z + w * y)],
        [2.0 * (x * y + w * z), 1.0 - 2.0 * (x * x + z * z), 2.0 * (y * z - w * x)],
        [2.0 * (x * z - w * y), 2.0 * (y * z + w * x), 1.0 - 2.0 * (x * x + y * y)],
    ]
    scales = [jnp.exp(rows[3 + k]) for k in range(3)]
    sx = [jx * (rot[0][j] - xn * rot[2][j]) for j in range(3)]
    sy = [jy * (rot[1][j] - yn * rot[2][j]) for j in range(3)]
    bx = [(sx[0] * rg[0][k] + sx[1] * rg[1][k] + sx[2] * rg[2][k]) * scales[k] for k in range(3)]
    by = [(sy[0] * rg[0][k] + sy[1] * rg[1][k] + sy[2] * rg[2][k]) * scales[k] for k in range(3)]
    cxx = bx[0] * bx[0] + bx[1] * bx[1] + bx[2] * bx[2] + 0.3
    cxy = bx[0] * by[0] + bx[1] * by[1] + bx[2] * by[2]
    cyy = by[0] * by[0] + by[1] * by[1] + by[2] * by[2] + 0.3
    inv_det = 1.0 / (cxx * cyy - cxy * cxy)
    opacity = 1.0 / (1.0 + jnp.exp(-rows[10]))
    view = [m[j] + (rot[0][j] * shift[0] + rot[1][j] * shift[1] + rot[2][j] * shift[2]) for j in range(3)]
    inv_len = 1.0 / jnp.sqrt(view[0] * view[0] + view[1] * view[1] + view[2] * view[2])
    dx, dy, dz = (t * inv_len for t in view)
    xx, yy, zz = dx * dx, dy * dy, dz * dz
    basis = [
        -sh_one * dy,
        sh_one * dz,
        -sh_one * dx,
        sh_two[0] * dx * dy,
        sh_two[1] * dy * dz,
        sh_two[2] * (2.0 * zz - xx - yy),
        sh_two[3] * dx * dz,
        sh_two[4] * (xx - yy),
        sh_three[0] * dy * (3.0 * xx - yy),
        sh_three[1] * dx * dy * dz,
        sh_three[2] * dy * (4.0 * zz - xx - yy),
        sh_three[3] * dz * (2.0 * zz - 3.0 * xx - 3.0 * yy),
        sh_three[4] * dx * (4.0 * zz - xx - yy),
        sh_three[5] * dz * (xx - yy),
        sh_three[6] * dx * (xx - 3.0 * yy),
    ]
    colour = []
    for c in range(3):
        total = 0.5 + sh_zero * rows[11 + c]
        for k in range(1, 16):
            total = total + basis[k - 1] * rows[11 + 3 * k + c]
        colour.append(total)
    return [u, v, cyy * inv_det, -cxy * inv_det, cxx * inv_det, *colour, opacity]


def split(value, parts):
    out = []
    for _ in range(parts - 1):
        piece = value.astype(BF16)
        out.append(piece)
        value = value - piece.astype(F32)
    out.append(value.astype(BF16))
    return out


def dot_nn(a, b, precision=None):
    return lax.dot_general(a, b, (((1,), (0,)), ((), ())), precision=precision, preferred_element_type=F32)


def dot_nt(a, b, precision=None):
    return lax.dot_general(a, b, (((1,), (1,)), ((), ())), precision=precision, preferred_element_type=F32)


def where_equal(a, b):
    return jnp.where(a == b, 1.0, 0.0).astype(BF16)


def iota(shape, dim):
    return lax.broadcasted_iota(jnp.int32, shape, dim)


def place(x, z, c):
    return (x * 16 + z) * 2 + c


def as_message(feats):
    blocks = [feats[:, k * 128 : (k + 1) * 128] for k in range(4)]
    both = jnp.concatenate(blocks + blocks, axis=0).T
    return jnp.where(iota((64, 128), 1) < 64, both[0:64], both[64:128])


def kernel(
    params,
    cam,
    send_rows,
    tiles,
    lists,
    counts,
    targets,
    grads,
    rendered,
    pv,
    tail,
    pq,
    gq,
    camx,
    p3,
    oh,
    gs,
    fs,
    msg,
    mid,
    got,
    turned,
    ohr,
    upper,
    lower,
    fe,
    al,
    lk,
    bf,
    ws,
    sw2,
    rs,
    rt,
    ge,
    st,
    sv,
    psem,
    qsem,
    osem,
    csend,
    crecv,
    zsend,
    zrecv,
    xsend,
    xrecv,
    ysend,
    yrecv,
):
    me, my = lax.axis_index("gauss"), lax.axis_index("img")
    mx, mz, mc = me // 32, (me // 2) % 16, me % 2
    far_first = [8, 7, 9, 6, 10, 5, 11, 4, 12, 3, 13, 2, 14, 1, 15]
    z_peers = [(mz + j) % 16 for j in far_first]
    x_peers = [((mx + j // 2) % 4, (mc + j) % 2) for j in (4, 5, 2, 3, 6, 7, 1)]
    y_peers = [(my + j) % 4 for j in (2, 1, 3)]

    barrier = pltpu.get_barrier_semaphore()
    for z in z_peers:
        pl.semaphore_signal(barrier, inc=1, device_id={"gauss": place(mx, z, mc)}, device_id_type=MESH)
    for x, c in x_peers:
        pl.semaphore_signal(barrier, inc=1, device_id={"gauss": place(x, mz, c)}, device_id_type=MESH)
    for y in y_peers:
        pl.semaphore_signal(barrier, inc=1, device_id={"img": y}, device_id_type=MESH)

    load = pltpu.make_async_copy(params, pv, psem)
    load.start()
    for block in range(8):
        columns = pl.ds(pl.multiple_of(my * QUARTER + block * 128, 128), 128)
        pltpu.make_async_copy(params.at[:, columns], pq.at[block], qsem).start()

    for k in range(16):
        camx[my, k : k + 1, :] = jnp.zeros((1, 128), F32) + cam[0, k]

    sent = send_rows[...]
    row = iota((16, ROWS), 0)
    pieces = jnp.where(row == 0, (sent >> 6).astype(F32), jnp.where(row == 1, (sent & 63).astype(F32), 0.0))
    column = iota((ROWS, ROWS), 1)
    natural = ((column & 63) << 3) | (((column >> 6) & 1) << 2) | (column >> 7)
    order = where_equal(iota((ROWS, ROWS), 0), natural)
    pieces = dot_nn(pieces.astype(BF16), order)
    chosen = pieces[0:1] * 64.0 + pieces[1:2]

    @pl.loop(0, 64)
    def _(j):
        start = pl.multiple_of(j * 64, 64)
        gauss = (iota((64, ROWS), 0) + start).astype(F32)
        oh[pl.ds(start, 64), :] = where_equal(gauss, chosen)

    tail[...] = jnp.zeros((8, G_DEV), F32)
    load.wait()

    @pl.loop(0, 16)
    def _(j):
        here = pl.ds(pl.multiple_of(j * 256, 256), 256)
        tail[0:3, here] = pv[56:PARAMS, here]
        whole = jnp.concatenate([pv[0:56, here], tail[:, here]], axis=0)
        for n, piece in enumerate(split(whole, 3)):
            p3[64 * n : 64 * (n + 1), here] = piece

    picked = dot_nn(p3[...], oh[...])
    gs[...] = picked[0:64] + picked[64:128] + picked[128:192]
    feats = project_rows([gs[f : f + 1, :] for f in range(PARAMS)], [cam[0, k] for k in range(16)])
    fs[8:16, :] = jnp.zeros((8, ROWS), F32)
    for f in range(FEATS):
        fs[f : f + 1, :] = feats[f]

    pl.semaphore_wait(barrier, 25)

    for n, y in enumerate(y_peers):
        pltpu.make_async_remote_copy(
            src_ref=camx.at[my], dst_ref=camx.at[my], send_sem=csend.at[n], recv_sem=crecv.at[n],
            device_id={"img": y}, device_id_type=MESH,
        ).start()

    def exchange(turn, while_sent):
        z_copies, x_copies = [], []
        for z in z_peers:
            copy = pltpu.make_async_remote_copy(
                src_ref=msg.at[turn, :, z], dst_ref=mid.at[turn, mz], send_sem=zsend.at[turn], recv_sem=zrecv.at[turn],
                device_id={"gauss": place(mx, z, mc)}, device_id_type=MESH,
            )
            copy.start()
        mid[turn, mz] = msg[turn, :, mz]
        while_sent()
        span = mid.at[turn, pl.ds(0, 15)]
        pltpu.make_async_copy(span, span, zrecv.at[turn]).wait()
        mine = mc * 4 + mx
        for x, c in x_peers:
            pltpu.make_async_remote_copy(
                src_ref=mid.at[turn, :, x], dst_ref=got.at[turn, mine], send_sem=xsend.at[turn], recv_sem=xrecv.at[turn],
                device_id={"gauss": place(x, mz, c)}, device_id_type=MESH,
            ).start()
        got[turn, mine] = mid[turn, :, mx]
        pltpu.make_async_copy(span, span, zsend.at[turn]).wait()
        span = got.at[turn, pl.ds(0, 7)]
        pltpu.make_async_copy(span, span, xrecv.at[turn]).wait()
        pltpu.make_async_copy(span, span, xsend.at[turn]).wait()
        turned[...] = got.reshape(256, 128)[turn * 128 : (turn + 1) * 128, :].T
        half = turned[pl.ds(pl.multiple_of(mc * 64, 64), 64), :]
        return jnp.concatenate([half[16 * k : 16 * (k + 1)] for k in range(4)], axis=1)

    def prepare():
        named = jnp.concatenate([lists[0, 0:1, :], lists[0, 1:2, :]], axis=1)
        named = ((named & 3) << 7) | (((named >> 2) & 1) << 6) | (named >> 3)

        @pl.loop(0, 8)
        def _(j):
            start = pl.multiple_of(j * 64, 64)
            ohr[pl.ds(start, 64), :] = where_equal(iota((64, ROWS), 0) + start, named)

        earlier = jnp.where(iota((LIST, LIST), 0) < iota((LIST, LIST), 1), 1.0, 0.0).astype(BF16)
        for n in range(3):
            upper[LIST * n : LIST * (n + 1), :] = earlier
        later = jnp.where(iota((LIST, LIST), 0) > iota((LIST, LIST), 1), 1.0, 0.0).astype(BF16)
        for n in range(2):
            lower[LIST * n : LIST * (n + 1), :] = later

    msg.reshape(128, 128)[0:64, :] = as_message(fs[...])
    received = exchange(0, prepare)

    listed = dot_nn(jnp.concatenate(split(received, 3), axis=0), ohr[...])
    fe[...] = listed[0:16] + listed[16:32] + listed[32:48]

    def entry(f, t):
        return fe[f : f + 1, t * LIST : (t + 1) * LIST]

    pixel = iota((16, LIST), 0).astype(F32)
    off_x, quad_x, cross, quad_y, origin_y, weight = [], [], [], [], [], []
    for t in range(2):
        tile = tiles[0, t]
        off_x.append(entry(0, t) - (pixel + ((tile & 15) * 16).astype(F32)))
        origin_y.append(entry(1, t) - ((tile >> 4) * 16).astype(F32))
        quad_x.append(-0.5 * entry(2, t) * off_x[t] * off_x[t])
        cross.append(-entry(3, t))
        quad_y.append(-0.5 * entry(4, t))
        weight.append(jnp.where(iota((1, LIST), 1) < counts[0, t], entry(8, t), 0.0))

    def pixels(t, j):
        return pl.ds(pl.multiple_of(t * 256 + j * 16, 16), 16)

    @pl.loop(0, 16)
    def _(j):
        for t in range(2):
            here = pixels(t, j)
            off_y = origin_y[t] - j.astype(F32)
            power = quad_x[t] + off_x[t] * (cross[t] * off_y) + quad_y[t] * off_y * off_y
            alpha = weight[t] * jnp.exp(power)
            al[here, :] = alpha
            for n, piece in enumerate(split(jnp.log(1.0 - alpha), 3)):
                lk[here, LIST * n : LIST * (n + 1)] = piece

    bf[...] = dot_nn(lk[...], upper[...])

    @pl.loop(0, 16)
    def _(j):
        for t in range(2):
            here = pixels(t, j)
            ws[here, :] = al[here, :] * jnp.exp(bf[here, :])

    grad_colour = []
    for t in range(2):
        shown = ws[t * 256 : (t + 1) * 256, :]
        colours = dot_nt(fe[:, t * LIST : (t + 1) * LIST], shown, HIGHEST)[5:8]
        rendered[0, t] = colours
        rs[t] = jnp.zeros((8, 256), F32)
        rs[t, 0:3, :] = colours - targets[0, t]
        rt[t * 256 : (t + 1) * 256, :] = rs[t].T
        grad_colour.append(dot_nn(rs[t], shown, HIGHEST))

    @pl.loop(0, 16)
    def _(j):
        for t in range(2):
            here = pixels(t, j)
            resid = rt[here, :]
            along = resid[:, 0:1] * entry(5, t) + resid[:, 1:2] * entry(6, t) + resid[:, 2:3] * entry(7, t)
            share = along * ws[here, :]
            ws[here, :] = share
            for n, piece in enumerate(split(share, 2)):
                sw2[here, LIST * n : LIST * (n + 1)] = piece

    bf[...] = dot_nn(sw2[...], lower[...])

    ge[8:16, :] = jnp.zeros((8, ROWS), F32)
    for t in range(2):

        def moments(j, carry):
            here = pixels(t, j)
            alpha = al[here, :]
            off_y = origin_y[t] - j.astype(F32)
            flow = ws[here, :] - bf[here, :] * (alpha / (1.0 - alpha))
            flow_y = flow * off_y
            return carry[0] + flow, carry[1] + flow_y, carry[2] + flow_y * off_y

        zero = jnp.zeros((16, LIST), F32)
        flow, flow_y, flow_yy = lax.fori_loop(0, 16, moments, (zero, zero, zero))

        def over(value):
            return jnp.sum(value, axis=0, keepdims=True)

        m_x, m_y = over(flow * off_x[t]), over(flow_y)
        a, b, c = entry(2, t), entry(3, t), entry(4, t)
        out = [
            -(a * m_x + b * m_y),
            -(b * m_x + c * m_y),
            -0.5 * over(flow * off_x[t] * off_x[t]),
            -over(flow_y * off_x[t]),
            -0.5 * over(flow_yy),
            grad_colour[t][0:1],
            grad_colour[t][1:2],
            grad_colour[t][2:3],
            over(flow) / entry(8, t),
        ]
        for f in range(FEATS):
            ge[f : f + 1, t * LIST : (t + 1) * LIST] = out[f]

    back = dot_nt(jnp.concatenate(split(ge[...], 2), axis=0), ohr[...])
    msg.reshape(128, 128)[64:128, :] = as_message(back[0:16] + back[16:32])
    returned = exchange(1, lambda: None)
    returned = jnp.concatenate(split(returned, 2), axis=0)

    for n, q in enumerate(y_peers + [my]):
        part = dot_nt(returned, oh[pl.ds(pl.multiple_of(q * QUARTER, QUARTER), QUARTER), :])
        part = part[0:16] + part[16:32]
        for block in range(8):
            value = part[0:FEATS, block * 128 : (block + 1) * 128]
            if n < 3:
                st[n, :, block, :] = value
            else:
                sv[my, :, block, :] = value
        if n < 3:
            pltpu.make_async_remote_copy(
                src_ref=st.at[n], dst_ref=sv.at[my], send_sem=ysend.at[n], recv_sem=yrecv.at[n],
                device_id={"img": q}, device_id_type=MESH,
            ).start()

    pltpu.make_async_copy(pq, pq, qsem).wait()
    for n in range(3):
        pltpu.make_async_copy(camx.at[0], camx.at[0], csend.at[n]).wait()
        pltpu.make_async_copy(camx.at[0], camx.at[0], crecv.at[n]).wait()
    gq[...] = jnp.zeros((8, PARAMS, 128), F32)
    for n in range(3):
        pltpu.make_async_copy(st.at[n], st.at[n], yrecv.at[n]).wait()

    @pl.loop(0, 4)
    def _(view):
        camera = [jnp.broadcast_to(camx[view, k : k + 1, :], (8, 128)) for k in range(16)]
        _, pull = jax.vjp(lambda rows: project_rows(rows, camera), [pq[:, f, :] for f in range(PARAMS)])
        (out,) = pull([sv[view, f] for f in range(FEATS)])
        for f in range(PARAMS):
            gq[:, f, :] += out[f]

    for block in range(8):
        pltpu.make_async_copy(gq.at[block], grads.at[:, pl.ds(block * 128, 128)], osem).start()
    for n in range(3):
        pltpu.make_async_copy(st.at[n], st.at[n], ysend.at[n]).wait()
    pltpu.make_async_copy(gq, gq, osem).wait()


def local(params, cameras, send_rows, tile_ids, lists, counts, targets):
    vmem, smem, hbm = (pl.BlockSpec(memory_space=s) for s in (pltpu.VMEM, pltpu.SMEM, pl.ANY))
    dma = pltpu.SemaphoreType.DMA
    return pl.pallas_call(
        kernel,
        out_shape=(
            jax.ShapeDtypeStruct((PARAMS, QUARTER), F32),
            jax.ShapeDtypeStruct((1, 2, 3, 256), F32),
        ),
        in_specs=[hbm, smem, vmem, smem, vmem, smem, vmem],
        out_specs=(hbm, vmem),
        scratch_shapes=[
            pltpu.VMEM((PARAMS, G_DEV), F32),
            pltpu.VMEM((8, G_DEV), F32),
            pltpu.VMEM((8, PARAMS, 128), F32),
            pltpu.VMEM((8, PARAMS, 128), F32),
            pltpu.VMEM((4, 16, 128), F32),
            pltpu.VMEM((192, G_DEV), BF16),
            pltpu.VMEM((G_DEV, ROWS), BF16),
            pltpu.VMEM((64, ROWS), F32),
            pltpu.VMEM((16, ROWS), F32),
            pltpu.VMEM((2, 4, 16, 1, 128), F32),
            pltpu.VMEM((2, 16, 4, 1, 128), F32),
            pltpu.VMEM((2, 8, 16, 1, 128), F32),
            pltpu.VMEM((128, 128), F32),
            pltpu.VMEM((ROWS, ROWS), BF16),
            pltpu.VMEM((3 * LIST, LIST), BF16),
            pltpu.VMEM((2 * LIST, LIST), BF16),
            pltpu.VMEM((16, ROWS), F32),
            pltpu.VMEM((512, LIST), F32),
            pltpu.VMEM((512, 3 * LIST), BF16),
            pltpu.VMEM((512, LIST), F32),
            pltpu.VMEM((512, LIST), F32),
            pltpu.VMEM((512, 2 * LIST), BF16),
            pltpu.VMEM((2, 8, 256), F32),
            pltpu.VMEM((512, 8), F32),
            pltpu.VMEM((16, ROWS), F32),
            pltpu.VMEM((3, FEATS, 8, 128), F32),
            pltpu.VMEM((4, FEATS, 8, 128), F32),
            dma,
            dma,
            dma,
            dma((3,)),
            dma((3,)),
            dma((2,)),
            dma((2,)),
            dma((2,)),
            dma((2,)),
            dma((3,)),
            dma((3,)),
        ],
        compiler_params=pltpu.CompilerParams(
            collective_id=0, has_side_effects=True, vmem_limit_bytes=40 * 1024 * 1024
        ),
    )(params, cameras, send_rows, tile_ids, lists, counts, targets)


def solution(mesh):
    placed = (
        P(None, "gauss"),
        P("img", None),
        P("img", "gauss"),
        P("img", "gauss"),
        P("img", "gauss", None),
        P("img", "gauss"),
        P("img", "gauss", None, None),
    )
    return jax.shard_map(
        local,
        mesh=mesh,
        in_specs=placed,
        out_specs=(P(None, ("gauss", "img")), P("img", "gauss", None, None)),
        check_vma=False,
    )
```

```python
import jax
import jax.numpy as jnp
from jax import lax
from jax.experimental import pallas as pl
from jax.experimental.pallas import tpu as pltpu
from jax.sharding import PartitionSpec as P

MESH = pl.DeviceIdType.MESH
F32 = jnp.float32
BF16 = jnp.bfloat16
HIGHEST = lax.Precision.HIGHEST

FEATS = 9
PARAMS = 59
G_DEV = 4096
QUARTER = 1024
ROWS = 512
LIST = 256

sh_zero = 0.28209479177387814
sh_one = 0.4886025119029199
sh_two = [1.0925484305920792, -1.0925484305920792, 0.31539156525252005, -1.0925484305920792, 0.5462742152960396]
sh_three = [
    -0.5900435899266435,
    2.890611442640554,
    -0.4570457994644658,
    0.3731763325901154,
    -0.4570457994644658,
    1.445305721320277,
    -0.5900435899266435,
]


def project_rows(rows, camera):
    m = rows[0:3]
    rot = [[camera[3 * i + j] for j in range(3)] for i in range(3)]
    shift = camera[9:12]
    focal_x, focal_y, centre_x, centre_y = camera[12:16]
    p = [rot[i][0] * m[0] + rot[i][1] * m[1] + rot[i][2] * m[2] + shift[i] for i in range(3)]
    inv_z = 1.0 / p[2]
    xn, yn = p[0] * inv_z, p[1] * inv_z
    u = focal_x * xn + centre_x
    v = focal_y * yn + centre_y
    jx, jy = focal_x * inv_z, focal_y * inv_z
    q = rows[6:10]
    inv_q = 1.0 / jnp.sqrt(q[0] * q[0] + q[1] * q[1] + q[2] * q[2] + q[3] * q[3])
    w, x, y, z = (t * inv_q for t in q)
    rg = [
        [1.0 - 2.0 * (y * y + z * z), 2.0 * (x * y - w * z), 2.0 * (x * z + w * y)],
        [2.0 * (x * y + w * z), 1.0 - 2.0 * (x * x + z * z), 2.0 * (y * z - w * x)],
        [2.0 * (x * z - w * y), 2.0 * (y * z + w * x), 1.0 - 2.0 * (x * x + y * y)],
    ]
    scales = [jnp.exp(rows[3 + k]) for k in range(3)]
    sx = [jx * (rot[0][j] - xn * rot[2][j]) for j in range(3)]
    sy = [jy * (rot[1][j] - yn * rot[2][j]) for j in range(3)]
    bx = [(sx[0] * rg[0][k] + sx[1] * rg[1][k] + sx[2] * rg[2][k]) * scales[k] for k in range(3)]
    by = [(sy[0] * rg[0][k] + sy[1] * rg[1][k] + sy[2] * rg[2][k]) * scales[k] for k in range(3)]
    cxx = bx[0] * bx[0] + bx[1] * bx[1] + bx[2] * bx[2] + 0.3
    cxy = bx[0] * by[0] + bx[1] * by[1] + bx[2] * by[2]
    cyy = by[0] * by[0] + by[1] * by[1] + by[2] * by[2] + 0.3
    inv_det = 1.0 / (cxx * cyy - cxy * cxy)
    opacity = 1.0 / (1.0 + jnp.exp(-rows[10]))
    view = [m[j] + (rot[0][j] * shift[0] + rot[1][j] * shift[1] + rot[2][j] * shift[2]) for j in range(3)]
    inv_len = 1.0 / jnp.sqrt(view[0] * view[0] + view[1] * view[1] + view[2] * view[2])
    dx, dy, dz = (t * inv_len for t in view)
    xx, yy, zz = dx * dx, dy * dy, dz * dz
    basis = [
        -sh_one * dy,
        sh_one * dz,
        -sh_one * dx,
        sh_two[0] * dx * dy,
        sh_two[1] * dy * dz,
        sh_two[2] * (2.0 * zz - xx - yy),
        sh_two[3] * dx * dz,
        sh_two[4] * (xx - yy),
        sh_three[0] * dy * (3.0 * xx - yy),
        sh_three[1] * dx * dy * dz,
        sh_three[2] * dy * (4.0 * zz - xx - yy),
        sh_three[3] * dz * (2.0 * zz - 3.0 * xx - 3.0 * yy),
        sh_three[4] * dx * (4.0 * zz - xx - yy),
        sh_three[5] * dz * (xx - yy),
        sh_three[6] * dx * (xx - 3.0 * yy),
    ]
    colour = []
    for c in range(3):
        total = 0.5 + sh_zero * rows[11 + c]
        for k in range(1, 16):
            total = total + basis[k - 1] * rows[11 + 3 * k + c]
        colour.append(total)
    return [u, v, cyy * inv_det, -cxy * inv_det, cxx * inv_det, *colour, opacity]


def split(value, parts):
    out = []
    for _ in range(parts - 1):
        piece = value.astype(BF16)
        out.append(piece)
        value = value - piece.astype(F32)
    out.append(value.astype(BF16))
    return out


def dot_nn(a, b, precision=None):
    return lax.dot_general(a, b, (((1,), (0,)), ((), ())), precision=precision, preferred_element_type=F32)


def dot_nt(a, b, precision=None):
    return lax.dot_general(a, b, (((1,), (1,)), ((), ())), precision=precision, preferred_element_type=F32)


def where_equal(a, b):
    return jnp.where(a == b, 1.0, 0.0).astype(BF16)


def iota(shape, dim):
    return lax.broadcasted_iota(jnp.int32, shape, dim)


def place(x, z, c):
    return (x * 16 + z) * 2 + c


def as_message(feats):
    blocks = [feats[:, k * 128 : (k + 1) * 128] for k in range(4)]
    both = jnp.concatenate(blocks + blocks, axis=0).T
    return jnp.where(iota((64, 128), 1) < 64, both[0:64], both[64:128])


def as_columns(rows):
    both = jnp.concatenate([rows, rows], axis=0).T
    left = iota((16, 128), 1) < 64
    blocks = [jnp.where(left, both[16 * k : 16 * k + 16], both[64 + 16 * k : 80 + 16 * k]) for k in range(4)]
    return jnp.concatenate(blocks, axis=1)


def natural(column, received):
    k = column >> 7
    if received:
        x, c = (column >> 3) & 3, (column >> 5) & 1
        z = ((column >> 6) & 1) * 8 + (column & 7)
    else:
        x, c, z = (column >> 4) & 3, (column >> 6) & 1, column & 15
    return x * 128 + z * 8 + c * 4 + k


def column_of(row):
    return ((row & 3) << 7) | (((row >> 2) & 1) << 6) | (row >> 3)


def reorder(values, received):
    n = len(values)
    row = iota((16, ROWS), 0)
    pieces = jnp.zeros((16, ROWS), F32)
    for i, value in enumerate(values):
        pieces = jnp.where(row == 2 * i, (value >> 6).astype(F32), pieces)
        pieces = jnp.where(row == 2 * i + 1, (value & 63).astype(F32), pieces)
    order = where_equal(iota((ROWS, ROWS), 0), natural(iota((ROWS, ROWS), 1), received))
    pieces = dot_nn(pieces.astype(BF16), order)
    return [pieces[2 * i : 2 * i + 1] * 64.0 + pieces[2 * i + 1 : 2 * i + 2] for i in range(n)]


def kernel(
    params,
    cam_in,
    send_rows_in,
    tiles_in,
    lists_in,
    counts_in,
    targets_in,
    gq,
    rendered,
    cam,
    send_rows,
    tiles,
    lists,
    counts,
    targets,
    lsem,
    pv,
    tail,
    pq,
    info,
    p3,
    oh,
    high,
    low,
    gs,
    fs,
    msg,
    mid,
    comp,
    got,
    ohr,
    upper,
    lower,
    fe,
    al,
    lk,
    bf,
    ws,
    sw2,
    rs,
    ge,
    psem,
    isend,
    irecv,
    zsend,
    zrecv,
    xsend,
    xrecv,
    near_sem,
    view_sem,
):
    me, my = lax.axis_index("gauss"), lax.axis_index("img")
    mx, mz, mc = me // 32, (me // 2) % 16, me % 2
    far_first = [8, 7, 9, 6, 10, 5, 11, 4, 12, 3, 13, 2, 14, 1, 15]
    z_peers = [(mz + j) % 16 for j in far_first]
    z_near = z_peers[7:]
    x_peers = [((mx + x) % 4, (mc + c) % 2) for x in (2, 1, 3, 0) for c in (0, 1)]
    x_others = x_peers[:6] + x_peers[7:]
    y_peers = [(my + y) % 4 for y in (2, 1, 3)]

    def tell(semaphore, device):
        pl.semaphore_signal(semaphore, inc=1, device_id=device, device_id_type=MESH)

    barrier = pltpu.get_barrier_semaphore()
    for z in z_near[:2]:
        tell(barrier, {"gauss": place(mx, z, mc)})
    for x, c in x_others:
        tell(barrier, {"gauss": place(x, mz, c)})
    for z in z_near[2:]:
        tell(barrier, {"gauss": place(mx, z, mc)})
    for y in y_peers:
        tell(barrier, {"img": y})

    loads = [
        pltpu.make_async_copy(source, target, lsem.at[n])
        for n, (source, target) in enumerate(
            [(send_rows_in, send_rows), (cam_in, cam), (lists_in, lists)]
            + [(tiles_in, tiles), (counts_in, counts), (targets_in, targets)]
        )
    ]
    loads[0].start()
    for part in range(4):
        columns = pl.ds(part * QUARTER, QUARTER)
        pltpu.make_async_copy(params.at[:, columns], pv.at[:, columns], psem).start()
    for copy in loads[1:]:
        copy.start()
    loads[0].wait()

    (chosen,) = reorder([send_rows[...]], False)

    @pl.loop(0, 64)
    def _(j):
        start = pl.multiple_of(j * 64, 64)
        gauss = (iota((64, ROWS), 0) + start).astype(F32)
        oh[pl.ds(start, 64), :] = where_equal(gauss, chosen)

    tail[...] = jnp.zeros((8, G_DEV), F32)
    pltpu.make_async_copy(params, pv, psem).wait()
    for copy in loads[1:]:
        copy.wait()

    @pl.loop(0, 16)
    def _(j):
        here = pl.ds(pl.multiple_of(j * 256, 256), 256)
        tail[0:3, here] = pv[56:PARAMS, here]
        whole = jnp.concatenate([pv[0:56, here], tail[:, here]], axis=0)
        for n, piece in enumerate(split(whole, 3)):
            p3[64 * n : 64 * (n + 1), here] = piece

    picked = dot_nn(p3[...], oh[...])
    gs[...] = picked[0:64] + picked[64:128] + picked[128:192]
    feats = project_rows([gs[f : f + 1, :] for f in range(PARAMS)], [cam[0, k] for k in range(16)])
    fs[8:16, :] = jnp.zeros((8, ROWS), F32)
    for f in range(FEATS):
        fs[f : f + 1, :] = feats[f]

    pl.semaphore_wait(barrier, 18)
    for z in z_near:
        tell(near_sem, {"gauss": place(mx, z, mc)})
    for y in y_peers:
        tell(view_sem, {"img": y})

    left = iota((8, 128), 1) < 64
    mine = mc * 4 + mx

    def halves(first, second):
        return jnp.where(left, first, pltpu.roll(second, 64, 1)), jnp.where(left, pltpu.roll(first, 64, 1), second)

    def send_z(turn):
        for z in z_peers:
            pltpu.make_async_remote_copy(
                src_ref=msg.at[turn, :, z], dst_ref=mid.at[turn, :, mz], send_sem=zsend.at[turn], recv_sem=zrecv.at[turn],
                device_id={"gauss": place(mx, z, mc)}, device_id_type=MESH,
            ).start()
        mid[turn, :, mz] = msg[turn, :, mz]

    def wait_z(turn, sems):
        span = mid.at[turn, :, pl.ds(0, 15)]
        pltpu.make_async_copy(span, span, sems.at[turn]).wait()

    def send_x(turn, y, slot):
        for x, c in x_peers if y is not my else x_others:
            pltpu.make_async_remote_copy(
                src_ref=comp.at[turn, c * 4 + x], dst_ref=got.at[slot, mine], send_sem=xsend.at[turn],
                recv_sem=xrecv.at[slot], device_id={"gauss": place(x, mz, c), "img": y}, device_id_type=MESH,
            ).start()
        if y is my:
            got[slot, mine] = comp[turn, mine]

    def wait_x(slot, count):
        span = got.at[slot, pl.ds(0, count)]
        pltpu.make_async_copy(span, span, xrecv.at[slot]).wait()

    def prepare():
        named = jnp.concatenate([lists[0, 0:1, :], lists[0, 1:2, :]], axis=1)
        named = column_of(named)

        @pl.loop(0, 8)
        def _(j):
            start = pl.multiple_of(j * 64, 64)
            ohr[pl.ds(start, 64), :] = where_equal(iota((64, ROWS), 0) + start, named)

        earlier = jnp.where(iota((LIST, LIST), 0) < iota((LIST, LIST), 1), 1.0, 0.0).astype(BF16)
        later = jnp.where(iota((LIST, LIST), 0) > iota((LIST, LIST), 1), 1.0, 0.0).astype(BF16)
        for n in range(2):
            upper[LIST * n : LIST * (n + 1), :] = earlier
            lower[LIST * n : LIST * (n + 1), :] = later
        rs[...] = jnp.zeros((2, 16, 256), F32)
        ge[8:16, :] = jnp.zeros((8, ROWS), F32)

    packed = as_message(fs[...])
    for x in range(4):
        comp[0, x], comp[0, 4 + x] = halves(packed[16 * x : 16 * x + 8], packed[16 * x + 8 : 16 * x + 16])
    send_x(0, my, 4)
    for k in range(16):
        info[my, k : k + 1, :] = jnp.zeros((1, 128), F32) + cam[0, k]
    for k in range(4):
        info[my, 16 + k : 17 + k, :] = send_rows[:, k * 128 : (k + 1) * 128].astype(F32)
    info[my, 20:24, :] = jnp.zeros((4, 128), F32)
    for n, y in enumerate(y_peers):
        pltpu.make_async_remote_copy(
            src_ref=info.at[my], dst_ref=info.at[my], send_sem=isend.at[n], recv_sem=irecv.at[n],
            device_id={"img": y}, device_id_type=MESH,
        ).start()
    wait_x(4, 7)
    for x in range(4):
        low_z, high_z = halves(got[4, x], got[4, 4 + x])
        msg.reshape(128, 128)[16 * x : 16 * x + 8, :] = low_z
        msg.reshape(128, 128)[16 * x + 8 : 16 * x + 16, :] = high_z
    pl.semaphore_wait(near_sem, 8)
    send_z(0)
    prepare()
    wait_z(0, zrecv)
    received = as_columns(mid.reshape(128, 128)[0:64, :])

    listed = dot_nn(jnp.concatenate(split(received, 3), axis=0), ohr[...])
    fe[...] = listed[0:16] + listed[16:32] + listed[32:48]

    def entry(f, t):
        return fe[f : f + 1, t * LIST : (t + 1) * LIST]

    pixel = iota((16, LIST), 0).astype(F32)
    off_x, quad_x, cross, quad_y, origin_y, weight = [], [], [], [], [], []
    for t in range(2):
        tile = tiles[0, t]
        off_x.append(entry(0, t) - (pixel + ((tile & 15) * 16).astype(F32)))
        origin_y.append(entry(1, t) - ((tile >> 4) * 16).astype(F32))
        quad_x.append(-0.5 * entry(2, t) * off_x[t] * off_x[t])
        cross.append(-entry(3, t))
        quad_y.append(-0.5 * entry(4, t))
        weight.append(jnp.where(iota((1, LIST), 1) < counts[0, t], entry(8, t), 0.0))

    def pixels(t, j):
        return pl.ds(pl.multiple_of(t * 256 + j * 16, 16), 16)

    @pl.loop(0, 16, unroll=16)
    def _(j):
        for t in range(2):
            here = pixels(t, j)
            off_y = origin_y[t] - lax.convert_element_type(j, F32)
            power = quad_x[t] + off_x[t] * (cross[t] * off_y) + quad_y[t] * off_y * off_y
            alpha = weight[t] * jnp.exp(power)
            al[here, :] = alpha
            for n, piece in enumerate(split(jnp.log(1.0 - alpha), 2)):
                lk[here, LIST * n : LIST * (n + 1)] = piece

    bf[...] = dot_nn(lk[...], upper[...])

    @pl.loop(0, 16, unroll=16)
    def _(j):
        for t in range(2):
            here = pixels(t, j)
            ws[here, :] = al[here, :] * jnp.exp(bf[here, :])

    grad_colour = []
    for t in range(2):
        shown = split(ws[t * 256 : (t + 1) * 256, :], 3)
        tints = split(fe[:, t * LIST : (t + 1) * LIST], 3)
        stacked = jnp.concatenate(tints, axis=0)
        colours = dot_nt(stacked, shown[0]) + dot_nt(stacked, shown[1]) + dot_nt(stacked, shown[2])
        colours = (colours[0:16] + colours[16:32] + colours[32:48])[5:8]
        rendered[0, :, t, :] = colours
        rs[t, 5:8, :] = colours - targets[0, :, t, :]
        resid = split(rs[t], 2)
        stacked = jnp.concatenate(resid, axis=0)
        tinted = dot_nn(stacked, shown[0]) + dot_nn(stacked, shown[1])
        grad_colour.append(tinted[5:8] + tinted[21:24])
        resid = [piece.astype(F32) for piece in resid]
        turned = jnp.concatenate([resid[0], resid[1], resid[0]], axis=0).T.astype(BF16)
        bf[t * 256 : (t + 1) * 256, :] = dot_nn(turned, jnp.concatenate([tints[0], tints[0], tints[1]], axis=0))

    @pl.loop(0, 16, unroll=16)
    def _(j):
        for t in range(2):
            here = pixels(t, j)
            share = bf[here, :] * ws[here, :]
            ws[here, :] = share
            for n, piece in enumerate(split(share, 2)):
                sw2[here, LIST * n : LIST * (n + 1)] = piece

    bf[...] = dot_nn(sw2[...], lower[...])

    for t in range(2):

        def moments(j, carry):
            here = pixels(t, j)
            alpha = al[here, :]
            off_y = origin_y[t] - lax.convert_element_type(j, F32)
            flow = ws[here, :] - bf[here, :] * (alpha / (1.0 - alpha))
            flow_y = flow * off_y
            return carry[0] + flow, carry[1] + flow_y, carry[2] + flow_y * off_y

        zero = jnp.zeros((16, LIST), F32)
        flow, flow_y, flow_yy = lax.fori_loop(0, 16, moments, (zero, zero, zero), unroll=16)

        def over(value):
            return jnp.sum(value, axis=0, keepdims=True)

        m_x, m_y = over(flow * off_x[t]), over(flow_y)
        a, b, c = entry(2, t), entry(3, t), entry(4, t)
        out = [
            -(a * m_x + b * m_y),
            -(b * m_x + c * m_y),
            -0.5 * over(flow * off_x[t] * off_x[t]),
            -over(flow_y * off_x[t]),
            -0.5 * over(flow_yy),
            grad_colour[t][0:1],
            grad_colour[t][1:2],
            grad_colour[t][2:3],
            over(flow) / entry(8, t),
        ]
        for f in range(FEATS):
            ge[f : f + 1, t * LIST : (t + 1) * LIST] = out[f]

    back = dot_nt(jnp.concatenate(split(ge[...], 2), axis=0), ohr[...])
    msg.reshape(128, 128)[64:128, :] = as_message(back[0:16] + back[16:32])
    pulls = []

    def look_ahead():
        for n in range(3):
            pltpu.make_async_copy(info.at[0], info.at[0], irecv.at[n]).wait()
            pltpu.make_async_copy(info.at[0], info.at[0], isend.at[n]).wait()
        rows = [
            jnp.concatenate([info[view, 16 + k : 17 + k, :] for k in range(4)], axis=1).astype(jnp.int32)
            for view in range(4)
        ]
        for view, picks in enumerate(reorder(rows, True)):
            place_in = (picks - (my * QUARTER).astype(F32)).astype(jnp.int32)
            high[view] = jnp.where(iota((8, ROWS), 0) == (place_in >> 7), 1.0, 0.0)
            low[view] = where_equal(iota((128, ROWS), 0), place_in & 127)
        for block in range(8):
            pq[block] = pv[:, pl.ds(pl.multiple_of(my * QUARTER + block * 128, 128), 128)]
        own = [pq[:, f, :] for f in range(PARAMS)]
        for view in [my] + y_peers:
            camera = [jnp.broadcast_to(info[view, k : k + 1, :], (8, 128)) for k in range(16)]
            pulls.append(jax.vjp(lambda rows, camera=camera: project_rows(rows, camera), own)[1])

    send_z(1)
    look_ahead()
    wait_z(1, zrecv)
    for x in range(4):
        whole = mid.reshape(128, 128)[64 + 16 * x : 80 + 16 * x, :]
        comp[1, x], comp[1, 4 + x] = halves(whole[0:8], whole[8:16])
    pl.semaphore_wait(view_sem, 3)
    for y in y_peers + [my]:
        send_x(1, y, my)
    for turn in range(2):
        wait_z(turn, zsend)

    def pulled(view, number, count):
        wait_x(view, count)
        cols = as_columns(got[view].reshape(64, 128))
        parts = [high[view] * cols[f : f + 1] for f in range(FEATS)] + [jnp.zeros((8, ROWS), F32)]
        parts = split(jnp.concatenate(parts, axis=0), 2)
        sums = dot_nt(jnp.concatenate(parts, axis=0), low[view])
        sums = sums[0:80] + sums[80:160]
        (out,) = pulls[number]([sums[8 * f : 8 * f + 8] for f in range(FEATS)])
        return out

    total = pulled(my, 0, 7)
    for n, y in enumerate(y_peers):
        total = [a + b for a, b in zip(total, pulled(y, n + 1, 8))]
    for f in range(PARAMS):
        gq[:, f, :] = total[f]
    span = comp.at[0, pl.ds(0, 7)]
    pltpu.make_async_copy(span, span, xsend.at[0]).wait()
    span = got.at[0, pl.ds(0, 7)]
    pltpu.make_async_copy(span, span, xsend.at[1]).wait()
    span = got.at[pl.ds(0, 3)]
    pltpu.make_async_copy(span, span, xsend.at[1]).wait()


def finish(blocks, shown, grads, rendered, block, small, into, out):
    reads = [pltpu.make_async_copy(blocks.at[b], block.at[b], into.at[b]) for b in range(8)]
    reads.append(pltpu.make_async_copy(shown, small, into.at[8]))
    for copy in reads:
        copy.start()
    writes = [pltpu.make_async_copy(block.at[b], grads.at[:, pl.ds(b * 128, 128)], out.at[b]) for b in range(8)]
    writes.append(pltpu.make_async_copy(small, rendered, out.at[8]))
    for read, write in zip(reads, writes):
        read.wait()
        write.start()
    for write in writes:
        write.wait()


def local(params, cameras, send_rows, tile_ids, lists, counts, targets):
    vmem, anywhere = (pl.BlockSpec(memory_space=s) for s in (pltpu.VMEM, pl.ANY))
    dma = pltpu.SemaphoreType.DMA
    blocks, shown = pl.pallas_call(
        kernel,
        out_shape=(
            jax.ShapeDtypeStruct((8, PARAMS, 128), F32),
            jax.ShapeDtypeStruct((1, 3, 2, 256), F32),
        ),
        in_specs=[anywhere] * 7,
        out_specs=(vmem, vmem),
        scratch_shapes=[
            pltpu.SMEM((1, 16), F32),
            pltpu.VMEM((1, ROWS), jnp.int32),
            pltpu.SMEM((1, 2), jnp.int32),
            pltpu.VMEM((1, 2, LIST), jnp.int32),
            pltpu.SMEM((1, 2), jnp.int32),
            pltpu.VMEM((1, 3, 2, 256), F32),
            dma((6,)),
            pltpu.VMEM((PARAMS, G_DEV), F32),
            pltpu.VMEM((8, G_DEV), F32),
            pltpu.VMEM((8, PARAMS, 128), F32),
            pltpu.VMEM((4, 24, 128), F32),
            pltpu.VMEM((192, G_DEV), BF16),
            pltpu.VMEM((G_DEV, ROWS), BF16),
            pltpu.VMEM((4, 8, ROWS), F32),
            pltpu.VMEM((4, 128, ROWS), BF16),
            pltpu.VMEM((64, ROWS), F32),
            pltpu.VMEM((16, ROWS), F32),
            pltpu.VMEM((2, 4, 16, 1, 128), F32),
            pltpu.VMEM((2, 4, 16, 1, 128), F32),
            pltpu.VMEM((2, 8, 8, 128), F32),
            pltpu.VMEM((5, 8, 8, 128), F32),
            pltpu.VMEM((ROWS, ROWS), BF16),
            pltpu.VMEM((2 * LIST, LIST), BF16),
            pltpu.VMEM((2 * LIST, LIST), BF16),
            pltpu.VMEM((16, ROWS), F32),
            pltpu.VMEM((512, LIST), F32),
            pltpu.VMEM((512, 2 * LIST), BF16),
            pltpu.VMEM((512, LIST), F32),
            pltpu.VMEM((512, LIST), F32),
            pltpu.VMEM((512, 2 * LIST), BF16),
            pltpu.VMEM((2, 16, 256), F32),
            pltpu.VMEM((16, ROWS), F32),
            dma,
            dma((3,)),
            dma((3,)),
            dma((2,)),
            dma((2,)),
            dma((2,)),
            dma((5,)),
            pltpu.SemaphoreType.REGULAR,
            pltpu.SemaphoreType.REGULAR,
        ],
        compiler_params=pltpu.CompilerParams(
            collective_id=0, has_side_effects=True, vmem_limit_bytes=60 * 1024 * 1024
        ),
    )(params, cameras, send_rows, tile_ids, lists, counts, jnp.transpose(targets, (0, 2, 1, 3)))
    grads, shown = pl.pallas_call(
        finish,
        out_shape=(
            jax.ShapeDtypeStruct((PARAMS, QUARTER), F32),
            jax.ShapeDtypeStruct((1, 3, 2, 256), F32),
        ),
        in_specs=[anywhere, anywhere],
        out_specs=(anywhere, anywhere),
        scratch_shapes=[
            pltpu.VMEM((8, PARAMS, 128), F32),
            pltpu.VMEM((1, 3, 2, 256), F32),
            dma((9,)),
            dma((9,)),
        ],
        compiler_params=pltpu.CompilerParams(vmem_limit_bytes=60 * 1024 * 1024),
    )(blocks, shown)
    return grads, jnp.transpose(shown, (0, 2, 1, 3))


def solution(mesh):
    placed = (
        P(None, "gauss"),
        P("img", None),
        P("img", "gauss"),
        P("img", "gauss"),
        P("img", "gauss", None),
        P("img", "gauss"),
        P("img", "gauss", None, None),
    )
    return jax.shard_map(
        local,
        mesh=mesh,
        in_specs=placed,
        out_specs=(P(None, ("gauss", "img")), P("img", "gauss", None, None)),
        check_vma=False,
    )
```

```python
import jax
import jax.numpy as jnp
from jax import lax
from jax.experimental import pallas as pl
from jax.experimental.pallas import tpu as pltpu
from jax.sharding import PartitionSpec as P

MESH = pl.DeviceIdType.MESH
F32 = jnp.float32
BF16 = jnp.bfloat16
HIGHEST = lax.Precision.HIGHEST

FEATS = 9
PARAMS = 59
G_DEV = 4096
QUARTER = 1024
ROWS = 512
LIST = 256

sh_zero = 0.28209479177387814
sh_one = 0.4886025119029199
sh_two = [1.0925484305920792, -1.0925484305920792, 0.31539156525252005, -1.0925484305920792, 0.5462742152960396]
sh_three = [
    -0.5900435899266435,
    2.890611442640554,
    -0.4570457994644658,
    0.3731763325901154,
    -0.4570457994644658,
    1.445305721320277,
    -0.5900435899266435,
]


def project_rows(rows, camera):
    m = rows[0:3]
    rot = [[camera[3 * i + j] for j in range(3)] for i in range(3)]
    shift = camera[9:12]
    focal_x, focal_y, centre_x, centre_y = camera[12:16]
    p = [rot[i][0] * m[0] + rot[i][1] * m[1] + rot[i][2] * m[2] + shift[i] for i in range(3)]
    inv_z = 1.0 / p[2]
    xn, yn = p[0] * inv_z, p[1] * inv_z
    u = focal_x * xn + centre_x
    v = focal_y * yn + centre_y
    jx, jy = focal_x * inv_z, focal_y * inv_z
    q = rows[6:10]
    inv_q = 1.0 / jnp.sqrt(q[0] * q[0] + q[1] * q[1] + q[2] * q[2] + q[3] * q[3])
    w, x, y, z = (t * inv_q for t in q)
    rg = [
        [1.0 - 2.0 * (y * y + z * z), 2.0 * (x * y - w * z), 2.0 * (x * z + w * y)],
        [2.0 * (x * y + w * z), 1.0 - 2.0 * (x * x + z * z), 2.0 * (y * z - w * x)],
        [2.0 * (x * z - w * y), 2.0 * (y * z + w * x), 1.0 - 2.0 * (x * x + y * y)],
    ]
    scales = [jnp.exp(rows[3 + k]) for k in range(3)]
    sx = [jx * (rot[0][j] - xn * rot[2][j]) for j in range(3)]
    sy = [jy * (rot[1][j] - yn * rot[2][j]) for j in range(3)]
    bx = [(sx[0] * rg[0][k] + sx[1] * rg[1][k] + sx[2] * rg[2][k]) * scales[k] for k in range(3)]
    by = [(sy[0] * rg[0][k] + sy[1] * rg[1][k] + sy[2] * rg[2][k]) * scales[k] for k in range(3)]
    cxx = bx[0] * bx[0] + bx[1] * bx[1] + bx[2] * bx[2] + 0.3
    cxy = bx[0] * by[0] + bx[1] * by[1] + bx[2] * by[2]
    cyy = by[0] * by[0] + by[1] * by[1] + by[2] * by[2] + 0.3
    inv_det = 1.0 / (cxx * cyy - cxy * cxy)
    opacity = 1.0 / (1.0 + jnp.exp(-rows[10]))
    view = [m[j] + (rot[0][j] * shift[0] + rot[1][j] * shift[1] + rot[2][j] * shift[2]) for j in range(3)]
    inv_len = 1.0 / jnp.sqrt(view[0] * view[0] + view[1] * view[1] + view[2] * view[2])
    dx, dy, dz = (t * inv_len for t in view)
    xx, yy, zz = dx * dx, dy * dy, dz * dz
    basis = [
        -sh_one * dy,
        sh_one * dz,
        -sh_one * dx,
        sh_two[0] * dx * dy,
        sh_two[1] * dy * dz,
        sh_two[2] * (2.0 * zz - xx - yy),
        sh_two[3] * dx * dz,
        sh_two[4] * (xx - yy),
        sh_three[0] * dy * (3.0 * xx - yy),
        sh_three[1] * dx * dy * dz,
        sh_three[2] * dy * (4.0 * zz - xx - yy),
        sh_three[3] * dz * (2.0 * zz - 3.0 * xx - 3.0 * yy),
        sh_three[4] * dx * (4.0 * zz - xx - yy),
        sh_three[5] * dz * (xx - yy),
        sh_three[6] * dx * (xx - 3.0 * yy),
    ]
    colour = []
    for c in range(3):
        total = 0.5 + sh_zero * rows[11 + c]
        for k in range(1, 16):
            total = total + basis[k - 1] * rows[11 + 3 * k + c]
        colour.append(total)
    return [u, v, cyy * inv_det, -cxy * inv_det, cxx * inv_det, *colour, opacity]


def split(value, parts):
    out = []
    for _ in range(parts - 1):
        piece = value.astype(BF16)
        out.append(piece)
        value = value - piece.astype(F32)
    out.append(value.astype(BF16))
    return out


def dot_nn(a, b, precision=None):
    return lax.dot_general(a, b, (((1,), (0,)), ((), ())), precision=precision, preferred_element_type=F32)


def dot_nt(a, b, precision=None):
    return lax.dot_general(a, b, (((1,), (1,)), ((), ())), precision=precision, preferred_element_type=F32)


def where_equal(a, b):
    return jnp.where(a == b, 1.0, 0.0).astype(BF16)


def iota(shape, dim):
    return lax.broadcasted_iota(jnp.int32, shape, dim)


def place(x, z, c):
    return (x * 16 + z) * 2 + c


def as_message(feats):
    blocks = [feats[:, k * 128 : (k + 1) * 128] for k in range(4)]
    both = jnp.concatenate(blocks + blocks, axis=0).T
    return jnp.where(iota((64, 128), 1) < 64, both[0:64], both[64:128])


def as_columns(rows):
    both = jnp.concatenate([rows, rows], axis=0).T
    left = iota((16, 128), 1) < 64
    blocks = [jnp.where(left, both[16 * k : 16 * k + 16], both[64 + 16 * k : 80 + 16 * k]) for k in range(4)]
    return jnp.concatenate(blocks, axis=1)


def natural(column, received):
    k = column >> 7
    if received:
        x, c = (column >> 3) & 3, (column >> 5) & 1
        z = ((column >> 6) & 1) * 8 + (column & 7)
    else:
        x, c, z = (column >> 4) & 3, (column >> 6) & 1, column & 15
    return x * 128 + z * 8 + c * 4 + k


def column_of(row):
    return ((row & 3) << 7) | (((row >> 2) & 1) << 6) | (row >> 3)


def reorder(values, received):
    n = len(values)
    row = iota((16, ROWS), 0)
    pieces = jnp.zeros((16, ROWS), F32)
    for i, value in enumerate(values):
        pieces = jnp.where(row == 2 * i, (value >> 6).astype(F32), pieces)
        pieces = jnp.where(row == 2 * i + 1, (value & 63).astype(F32), pieces)
    order = where_equal(iota((ROWS, ROWS), 0), natural(iota((ROWS, ROWS), 1), received))
    pieces = dot_nn(pieces.astype(BF16), order)
    return [pieces[2 * i : 2 * i + 1] * 64.0 + pieces[2 * i + 1 : 2 * i + 2] for i in range(n)]


def kernel(
    params,
    cam_in,
    send_rows_in,
    tiles_in,
    lists_in,
    counts_in,
    targets_in,
    gq,
    rendered,
    cam,
    send_rows,
    tiles,
    lists,
    counts,
    targets,
    lsem,
    pv,
    tail,
    pq,
    info,
    p3,
    oh,
    high,
    low,
    gs,
    fs,
    msg,
    mid,
    comp,
    got,
    ohr,
    upper,
    lower,
    fe,
    al,
    lk,
    bf,
    ws,
    sw2,
    rs,
    ge,
    psem,
    isend,
    irecv,
    zsend,
    zrecv,
    xsend,
    xrecv,
    near_sem,
    view_sem,
):
    me, my = lax.axis_index("gauss"), lax.axis_index("img")
    mx, mz, mc = me // 32, (me // 2) % 16, me % 2
    far_first = [8, 7, 9, 6, 10, 5, 11, 4, 12, 3, 13, 2, 14, 1, 15]
    z_peers = [(mz + j) % 16 for j in far_first]
    z_near = z_peers[7:]
    x_peers = [((mx + x) % 4, (mc + c) % 2) for x in (2, 1, 3, 0) for c in (0, 1)]
    x_others = x_peers[:6] + x_peers[7:]
    y_peers = [(my + y) % 4 for y in (2, 1, 3)]

    def tell(semaphore, device):
        pl.semaphore_signal(semaphore, inc=1, device_id=device, device_id_type=MESH)

    barrier = pltpu.get_barrier_semaphore()
    for z in z_near[:2]:
        tell(barrier, {"gauss": place(mx, z, mc)})
    for x, c in x_others:
        tell(barrier, {"gauss": place(x, mz, c)})
    for z in z_near[2:]:
        tell(barrier, {"gauss": place(mx, z, mc)})
    for y in y_peers:
        tell(barrier, {"img": y})

    loads = [
        pltpu.make_async_copy(source, target, lsem.at[n])
        for n, (source, target) in enumerate(
            [(send_rows_in, send_rows), (cam_in, cam), (lists_in, lists)]
            + [(tiles_in, tiles), (counts_in, counts), (targets_in, targets)]
        )
    ]
    loads[0].start()
    for part in range(4):
        columns = pl.ds(part * QUARTER, QUARTER)
        pltpu.make_async_copy(params.at[:, columns], pv.at[:, columns], psem).start()
    for copy in loads[1:]:
        copy.start()
    loads[0].wait()

    (chosen,) = reorder([send_rows[...]], False)

    @pl.loop(0, 64)
    def _(j):
        start = pl.multiple_of(j * 64, 64)
        gauss = (iota((64, ROWS), 0) + start).astype(F32)
        oh[pl.ds(start, 64), :] = where_equal(gauss, chosen)

    tail[...] = jnp.zeros((8, G_DEV), F32)
    pltpu.make_async_copy(params, pv, psem).wait()
    for copy in loads[1:]:
        copy.wait()

    @pl.loop(0, 16)
    def _(j):
        here = pl.ds(pl.multiple_of(j * 256, 256), 256)
        tail[0:3, here] = pv[56:PARAMS, here]
        whole = jnp.concatenate([pv[0:56, here], tail[:, here]], axis=0)
        for n, piece in enumerate(split(whole, 3)):
            p3[64 * n : 64 * (n + 1), here] = piece

    picked = dot_nn(p3[...], oh[...])
    gs[...] = picked[0:64] + picked[64:128] + picked[128:192]
    feats = project_rows([gs[f : f + 1, :] for f in range(PARAMS)], [cam[0, k] for k in range(16)])
    fs[8:16, :] = jnp.zeros((8, ROWS), F32)
    for f in range(FEATS):
        fs[f : f + 1, :] = feats[f]

    pl.semaphore_wait(barrier, 18)
    for z in z_near:
        tell(near_sem, {"gauss": place(mx, z, mc)})
    for y in y_peers:
        tell(view_sem, {"img": y})

    left = iota((8, 128), 1) < 64
    mine = mc * 4 + mx

    def halves(first, second):
        return jnp.where(left, first, pltpu.roll(second, 64, 1)), jnp.where(left, pltpu.roll(first, 64, 1), second)

    def send_z(turn):
        for z in z_peers:
            pltpu.make_async_remote_copy(
                src_ref=msg.at[turn, :, z], dst_ref=mid.at[turn, :, mz], send_sem=zsend.at[turn], recv_sem=zrecv.at[turn],
                device_id={"gauss": place(mx, z, mc)}, device_id_type=MESH,
            ).start()
        mid[turn, :, mz] = msg[turn, :, mz]

    def wait_z(turn, sems):
        span = mid.at[turn, :, pl.ds(0, 15)]
        pltpu.make_async_copy(span, span, sems.at[turn]).wait()

    def send_x(turn, y, slot):
        for x, c in x_peers if y is not my else x_others:
            pltpu.make_async_remote_copy(
                src_ref=comp.at[turn, c * 4 + x], dst_ref=got.at[slot, mine], send_sem=xsend.at[turn],
                recv_sem=xrecv.at[slot], device_id={"gauss": place(x, mz, c), "img": y}, device_id_type=MESH,
            ).start()
        if y is my:
            got[slot, mine] = comp[turn, mine]

    def wait_x(slot, count):
        span = got.at[slot, pl.ds(0, count)]
        pltpu.make_async_copy(span, span, xrecv.at[slot]).wait()

    def prepare():
        named = jnp.concatenate([lists[0, 0:1, :], lists[0, 1:2, :]], axis=1)
        named = column_of(named)

        @pl.loop(0, 8)
        def _(j):
            start = pl.multiple_of(j * 64, 64)
            ohr[pl.ds(start, 64), :] = where_equal(iota((64, ROWS), 0) + start, named)

        earlier = jnp.where(iota((LIST, LIST), 0) < iota((LIST, LIST), 1), 1.0, 0.0).astype(BF16)
        later = jnp.where(iota((LIST, LIST), 0) > iota((LIST, LIST), 1), 1.0, 0.0).astype(BF16)
        for n in range(2):
            upper[LIST * n : LIST * (n + 1), :] = earlier
            lower[LIST * n : LIST * (n + 1), :] = later
        rs[...] = jnp.zeros((2, 16, 256), F32)
        ge[8:16, :] = jnp.zeros((8, ROWS), F32)

    packed = as_message(fs[...])
    for x in range(4):
        comp[0, x], comp[0, 4 + x] = halves(packed[16 * x : 16 * x + 8], packed[16 * x + 8 : 16 * x + 16])
    send_x(0, my, 4)
    for k in range(16):
        info[my, k : k + 1, :] = jnp.zeros((1, 128), F32) + cam[0, k]
    for k in range(4):
        info[my, 16 + k : 17 + k, :] = send_rows[:, k * 128 : (k + 1) * 128].astype(F32)
    info[my, 20:24, :] = jnp.zeros((4, 128), F32)
    for n, y in enumerate(y_peers):
        pltpu.make_async_remote_copy(
            src_ref=info.at[my], dst_ref=info.at[my], send_sem=isend.at[n], recv_sem=irecv.at[n],
            device_id={"img": y}, device_id_type=MESH,
        ).start()
    wait_x(4, 7)
    for x in range(4):
        low_z, high_z = halves(got[4, x], got[4, 4 + x])
        msg.reshape(128, 128)[16 * x : 16 * x + 8, :] = low_z
        msg.reshape(128, 128)[16 * x + 8 : 16 * x + 16, :] = high_z
    pl.semaphore_wait(near_sem, 8)
    send_z(0)
    prepare()
    wait_z(0, zrecv)
    received = as_columns(mid.reshape(128, 128)[0:64, :])

    listed = dot_nn(jnp.concatenate(split(received, 3), axis=0), ohr[...])
    fe[...] = listed[0:16] + listed[16:32] + listed[32:48]

    def entry(f, t):
        return fe[f : f + 1, t * LIST : (t + 1) * LIST]

    pixel = iota((16, LIST), 0).astype(F32)
    off_x, quad_x, cross, quad_y, origin_y, weight = [], [], [], [], [], []
    for t in range(2):
        tile = tiles[0, t]
        off_x.append(entry(0, t) - (pixel + ((tile & 15) * 16).astype(F32)))
        origin_y.append(entry(1, t) - ((tile >> 4) * 16).astype(F32))
        quad_x.append(-0.5 * entry(2, t) * off_x[t] * off_x[t])
        cross.append(-entry(3, t))
        quad_y.append(-0.5 * entry(4, t))
        weight.append(jnp.where(iota((1, LIST), 1) < counts[0, t], entry(8, t), 0.0))

    def pixels(t, j):
        return pl.ds(pl.multiple_of(t * 256 + j * 16, 16), 16)

    @pl.loop(0, 16, unroll=16)
    def _(j):
        for t in range(2):
            here = pixels(t, j)
            off_y = origin_y[t] - lax.convert_element_type(j, F32)
            power = quad_x[t] + off_x[t] * (cross[t] * off_y) + quad_y[t] * off_y * off_y
            alpha = weight[t] * jnp.exp(power)
            al[here, :] = alpha
            for n, piece in enumerate(split(jnp.log(1.0 - alpha), 2)):
                lk[here, LIST * n : LIST * (n + 1)] = piece

    bf[...] = dot_nn(lk[...], upper[...])

    @pl.loop(0, 16, unroll=16)
    def _(j):
        for t in range(2):
            here = pixels(t, j)
            ws[here, :] = al[here, :] * jnp.exp(bf[here, :])

    grad_colour = []
    for t in range(2):
        shown = split(ws[t * 256 : (t + 1) * 256, :], 3)
        tints = split(fe[:, t * LIST : (t + 1) * LIST], 3)
        stacked = jnp.concatenate(tints, axis=0)
        colours = dot_nt(stacked, shown[0]) + dot_nt(stacked, shown[1]) + dot_nt(stacked, shown[2])
        colours = (colours[0:16] + colours[16:32] + colours[32:48])[5:8]
        rendered[0, :, t, :] = colours
        rs[t, 5:8, :] = colours - targets[0, :, t, :]
        resid = split(rs[t], 2)
        stacked = jnp.concatenate(resid, axis=0)
        tinted = dot_nn(stacked, shown[0]) + dot_nn(stacked, shown[1])
        grad_colour.append(tinted[5:8] + tinted[21:24])
        resid = [piece.astype(F32) for piece in resid]
        turned = jnp.concatenate([resid[0], resid[1], resid[0]], axis=0).T.astype(BF16)
        bf[t * 256 : (t + 1) * 256, :] = dot_nn(turned, jnp.concatenate([tints[0], tints[0], tints[1]], axis=0))

    @pl.loop(0, 16, unroll=16)
    def _(j):
        for t in range(2):
            here = pixels(t, j)
            share = bf[here, :] * ws[here, :]
            ws[here, :] = share
            for n, piece in enumerate(split(share, 2)):
                sw2[here, LIST * n : LIST * (n + 1)] = piece

    bf[...] = dot_nn(sw2[...], lower[...])

    for t in range(2):

        def moments(j, carry):
            here = pixels(t, j)
            alpha = al[here, :]
            off_y = origin_y[t] - lax.convert_element_type(j, F32)
            flow = ws[here, :] - bf[here, :] * (alpha / (1.0 - alpha))
            flow_y = flow * off_y
            return carry[0] + flow, carry[1] + flow_y, carry[2] + flow_y * off_y

        zero = jnp.zeros((16, LIST), F32)
        flow, flow_y, flow_yy = lax.fori_loop(0, 16, moments, (zero, zero, zero), unroll=16)

        def over(value):
            return jnp.sum(value, axis=0, keepdims=True)

        m_x, m_y = over(flow * off_x[t]), over(flow_y)
        a, b, c = entry(2, t), entry(3, t), entry(4, t)
        out = [
            -(a * m_x + b * m_y),
            -(b * m_x + c * m_y),
            -0.5 * over(flow * off_x[t] * off_x[t]),
            -over(flow_y * off_x[t]),
            -0.5 * over(flow_yy),
            grad_colour[t][0:1],
            grad_colour[t][1:2],
            grad_colour[t][2:3],
            over(flow) / entry(8, t),
        ]
        for f in range(FEATS):
            ge[f : f + 1, t * LIST : (t + 1) * LIST] = out[f]

    back = dot_nt(jnp.concatenate(split(ge[...], 2), axis=0), ohr[...])
    msg.reshape(128, 128)[64:128, :] = as_message(back[0:16] + back[16:32])
    pulls = []

    def look_ahead():
        for n in range(3):
            pltpu.make_async_copy(info.at[0], info.at[0], irecv.at[n]).wait()
            pltpu.make_async_copy(info.at[0], info.at[0], isend.at[n]).wait()
        rows = [
            jnp.concatenate([info[view, 16 + k : 17 + k, :] for k in range(4)], axis=1).astype(jnp.int32)
            for view in range(4)
        ]
        for view, picks in enumerate(reorder(rows, True)):
            place_in = (picks - (my * QUARTER).astype(F32)).astype(jnp.int32)
            high[view] = jnp.where(iota((8, ROWS), 0) == (place_in >> 7), 1.0, 0.0)
            low[view] = where_equal(iota((128, ROWS), 0), place_in & 127)
        for block in range(8):
            pq[block] = pv[:, pl.ds(pl.multiple_of(my * QUARTER + block * 128, 128), 128)]
        own = [pq[:, f, :] for f in range(PARAMS)]
        for view in [my] + y_peers:
            camera = [jnp.broadcast_to(info[view, k : k + 1, :], (8, 128)) for k in range(16)]
            pulls.append(jax.vjp(lambda rows, camera=camera: project_rows(rows, camera), own)[1])

    send_z(1)
    look_ahead()
    wait_z(1, zrecv)
    for x in range(4):
        whole = mid.reshape(128, 128)[64 + 16 * x : 80 + 16 * x, :]
        comp[1, x], comp[1, 4 + x] = halves(whole[0:8], whole[8:16])
    pl.semaphore_wait(view_sem, 3)
    for y in (y_peers[0], my, y_peers[1], y_peers[2]):
        send_x(1, y, my)
    for turn in range(2):
        wait_z(turn, zsend)

    def pulled(view, number, count):
        wait_x(view, count)
        cols = as_columns(got[view].reshape(64, 128))
        parts = [high[view] * cols[f : f + 1] for f in range(FEATS)] + [jnp.zeros((8, ROWS), F32)]
        parts = split(jnp.concatenate(parts, axis=0), 2)
        sums = dot_nt(jnp.concatenate(parts, axis=0), low[view])
        sums = sums[0:80] + sums[80:160]
        (out,) = pulls[number]([sums[8 * f : 8 * f + 8] for f in range(FEATS)])
        return out

    total = pulled(my, 0, 7)
    for n, y in ((1, y_peers[1]), (2, y_peers[2]), (0, y_peers[0])):
        total = [a + b for a, b in zip(total, pulled(y, n + 1, 8))]
    for f in range(PARAMS):
        gq[:, f, :] = total[f]
    span = comp.at[0, pl.ds(0, 7)]
    pltpu.make_async_copy(span, span, xsend.at[0]).wait()
    span = got.at[0, pl.ds(0, 7)]
    pltpu.make_async_copy(span, span, xsend.at[1]).wait()
    span = got.at[pl.ds(0, 3)]
    pltpu.make_async_copy(span, span, xsend.at[1]).wait()


def finish(blocks, shown, grads, rendered, sem):
    copies = [pltpu.make_async_copy(blocks.at[b], grads.at[:, pl.ds(b * 128, 128)], sem.at[b]) for b in range(8)]
    copies.append(pltpu.make_async_copy(shown, rendered, sem.at[8]))
    for copy in copies:
        copy.start()
    for copy in copies:
        copy.wait()


def local(params, cameras, send_rows, tile_ids, lists, counts, targets):
    vmem, anywhere = (pl.BlockSpec(memory_space=s) for s in (pltpu.VMEM, pl.ANY))
    dma = pltpu.SemaphoreType.DMA
    operands = (params, cameras, send_rows, tile_ids, lists, counts, jnp.transpose(targets, (0, 2, 1, 3)))
    blocks, shown = pl.pallas_call(
        kernel,
        out_shape=(
            jax.ShapeDtypeStruct((8, PARAMS, 128), F32),
            jax.ShapeDtypeStruct((1, 3, 2, 256), F32),
        ),
        in_specs=[anywhere] * 7,
        out_specs=(vmem, vmem),
        scratch_shapes=[
            pltpu.SMEM((1, 16), F32),
            pltpu.VMEM((1, ROWS), jnp.int32),
            pltpu.SMEM((1, 2), jnp.int32),
            pltpu.VMEM((1, 2, LIST), jnp.int32),
            pltpu.SMEM((1, 2), jnp.int32),
            pltpu.VMEM((1, 3, 2, 256), F32),
            dma((6,)),
            pltpu.VMEM((PARAMS, G_DEV), F32),
            pltpu.VMEM((8, G_DEV), F32),
            pltpu.VMEM((8, PARAMS, 128), F32),
            pltpu.VMEM((4, 24, 128), F32),
            pltpu.VMEM((192, G_DEV), BF16),
            pltpu.VMEM((G_DEV, ROWS), BF16),
            pltpu.VMEM((4, 8, ROWS), F32),
            pltpu.VMEM((4, 128, ROWS), BF16),
            pltpu.VMEM((64, ROWS), F32),
            pltpu.VMEM((16, ROWS), F32),
            pltpu.VMEM((2, 4, 16, 1, 128), F32),
            pltpu.VMEM((2, 4, 16, 1, 128), F32),
            pltpu.VMEM((2, 8, 8, 128), F32),
            pltpu.VMEM((5, 8, 8, 128), F32),
            pltpu.VMEM((ROWS, ROWS), BF16),
            pltpu.VMEM((2 * LIST, LIST), BF16),
            pltpu.VMEM((2 * LIST, LIST), BF16),
            pltpu.VMEM((16, ROWS), F32),
            pltpu.VMEM((512, LIST), F32),
            pltpu.VMEM((512, 2 * LIST), BF16),
            pltpu.VMEM((512, LIST), F32),
            pltpu.VMEM((512, LIST), F32),
            pltpu.VMEM((512, 2 * LIST), BF16),
            pltpu.VMEM((2, 16, 256), F32),
            pltpu.VMEM((16, ROWS), F32),
            dma,
            dma((3,)),
            dma((3,)),
            dma((2,)),
            dma((2,)),
            dma((2,)),
            dma((5,)),
            pltpu.SemaphoreType.REGULAR,
            pltpu.SemaphoreType.REGULAR,
        ],
        compiler_params=pltpu.CompilerParams(
            collective_id=0, has_side_effects=True, vmem_limit_bytes=32 * 1024 * 1024
        ),
    )(*(pltpu.with_memory_space_constraint(operand, pltpu.HBM) for operand in operands))
    grads, shown = pl.pallas_call(
        finish,
        out_shape=(
            jax.ShapeDtypeStruct((PARAMS, QUARTER), F32),
            jax.ShapeDtypeStruct((1, 3, 2, 256), F32),
        ),
        in_specs=[anywhere, anywhere],
        out_specs=(anywhere, anywhere),
        scratch_shapes=[dma((9,))],
    )(*(pltpu.with_memory_space_constraint(part, pltpu.VMEM) for part in (blocks, shown)))
    return grads, jnp.transpose(shown, (0, 2, 1, 3))


def solution(mesh):
    placed = (
        P(None, "gauss"),
        P("img", None),
        P("img", "gauss"),
        P("img", "gauss"),
        P("img", "gauss", None),
        P("img", "gauss"),
        P("img", "gauss", None, None),
    )
    return jax.shard_map(
        local,
        mesh=mesh,
        in_specs=placed,
        out_specs=(P(None, ("gauss", "img")), P("img", "gauss", None, None)),
        check_vma=False,
    )
```

```python
import jax
import jax.numpy as jnp
from jax import lax
from jax.experimental import pallas as pl
from jax.experimental.pallas import tpu as pltpu
from jax.sharding import PartitionSpec as P

MESH = pl.DeviceIdType.MESH
F32 = jnp.float32
BF16 = jnp.bfloat16
HIGHEST = lax.Precision.HIGHEST

FEATS = 9
PARAMS = 59
G_DEV = 4096
QUARTER = 1024
ROWS = 512
LIST = 256

sh_zero = 0.28209479177387814
sh_one = 0.4886025119029199
sh_two = [1.0925484305920792, -1.0925484305920792, 0.31539156525252005, -1.0925484305920792, 0.5462742152960396]
sh_three = [
    -0.5900435899266435,
    2.890611442640554,
    -0.4570457994644658,
    0.3731763325901154,
    -0.4570457994644658,
    1.445305721320277,
    -0.5900435899266435,
]


def project_rows(rows, camera):
    m = rows[0:3]
    rot = [[camera[3 * i + j] for j in range(3)] for i in range(3)]
    shift = camera[9:12]
    focal_x, focal_y, centre_x, centre_y = camera[12:16]
    p = [rot[i][0] * m[0] + rot[i][1] * m[1] + rot[i][2] * m[2] + shift[i] for i in range(3)]
    inv_z = 1.0 / p[2]
    xn, yn = p[0] * inv_z, p[1] * inv_z
    u = focal_x * xn + centre_x
    v = focal_y * yn + centre_y
    jx, jy = focal_x * inv_z, focal_y * inv_z
    q = rows[6:10]
    inv_q = 1.0 / jnp.sqrt(q[0] * q[0] + q[1] * q[1] + q[2] * q[2] + q[3] * q[3])
    w, x, y, z = (t * inv_q for t in q)
    rg = [
        [1.0 - 2.0 * (y * y + z * z), 2.0 * (x * y - w * z), 2.0 * (x * z + w * y)],
        [2.0 * (x * y + w * z), 1.0 - 2.0 * (x * x + z * z), 2.0 * (y * z - w * x)],
        [2.0 * (x * z - w * y), 2.0 * (y * z + w * x), 1.0 - 2.0 * (x * x + y * y)],
    ]
    scales = [jnp.exp(rows[3 + k]) for k in range(3)]
    sx = [jx * (rot[0][j] - xn * rot[2][j]) for j in range(3)]
    sy = [jy * (rot[1][j] - yn * rot[2][j]) for j in range(3)]
    bx = [(sx[0] * rg[0][k] + sx[1] * rg[1][k] + sx[2] * rg[2][k]) * scales[k] for k in range(3)]
    by = [(sy[0] * rg[0][k] + sy[1] * rg[1][k] + sy[2] * rg[2][k]) * scales[k] for k in range(3)]
    cxx = bx[0] * bx[0] + bx[1] * bx[1] + bx[2] * bx[2] + 0.3
    cxy = bx[0] * by[0] + bx[1] * by[1] + bx[2] * by[2]
    cyy = by[0] * by[0] + by[1] * by[1] + by[2] * by[2] + 0.3
    inv_det = 1.0 / (cxx * cyy - cxy * cxy)
    opacity = 1.0 / (1.0 + jnp.exp(-rows[10]))
    view = [m[j] + (rot[0][j] * shift[0] + rot[1][j] * shift[1] + rot[2][j] * shift[2]) for j in range(3)]
    inv_len = 1.0 / jnp.sqrt(view[0] * view[0] + view[1] * view[1] + view[2] * view[2])
    dx, dy, dz = (t * inv_len for t in view)
    xx, yy, zz = dx * dx, dy * dy, dz * dz
    basis = [
        -sh_one * dy,
        sh_one * dz,
        -sh_one * dx,
        sh_two[0] * dx * dy,
        sh_two[1] * dy * dz,
        sh_two[2] * (2.0 * zz - xx - yy),
        sh_two[3] * dx * dz,
        sh_two[4] * (xx - yy),
        sh_three[0] * dy * (3.0 * xx - yy),
        sh_three[1] * dx * dy * dz,
        sh_three[2] * dy * (4.0 * zz - xx - yy),
        sh_three[3] * dz * (2.0 * zz - 3.0 * xx - 3.0 * yy),
        sh_three[4] * dx * (4.0 * zz - xx - yy),
        sh_three[5] * dz * (xx - yy),
        sh_three[6] * dx * (xx - 3.0 * yy),
    ]
    colour = []
    for c in range(3):
        total = 0.5 + sh_zero * rows[11 + c]
        for k in range(1, 16):
            total = total + basis[k - 1] * rows[11 + 3 * k + c]
        colour.append(total)
    return [u, v, cyy * inv_det, -cxy * inv_det, cxx * inv_det, *colour, opacity]


def split(value, parts):
    out = []
    for _ in range(parts - 1):
        piece = value.astype(BF16)
        out.append(piece)
        value = value - piece.astype(F32)
    out.append(value.astype(BF16))
    return out


def dot_nn(a, b, precision=None):
    return lax.dot_general(a, b, (((1,), (0,)), ((), ())), precision=precision, preferred_element_type=F32)


def dot_nt(a, b, precision=None):
    return lax.dot_general(a, b, (((1,), (1,)), ((), ())), precision=precision, preferred_element_type=F32)


def where_equal(a, b):
    return jnp.where(a == b, 1.0, 0.0).astype(BF16)


def iota(shape, dim):
    return lax.broadcasted_iota(jnp.int32, shape, dim)


def place(x, z, c):
    return (x * 16 + z) * 2 + c


def as_message(feats):
    blocks = [feats[:, k * 128 : (k + 1) * 128] for k in range(4)]
    both = jnp.concatenate(blocks + blocks, axis=0).T
    return jnp.where(iota((64, 128), 1) < 64, both[0:64], both[64:128])


def as_columns(rows):
    both = jnp.concatenate([rows, rows], axis=0).T
    left = iota((16, 128), 1) < 64
    blocks = [jnp.where(left, both[16 * k : 16 * k + 16], both[64 + 16 * k : 80 + 16 * k]) for k in range(4)]
    return jnp.concatenate(blocks, axis=1)


def natural(column, received):
    k = column >> 7
    if received:
        x, c = (column >> 3) & 3, (column >> 5) & 1
        z = ((column >> 6) & 1) * 8 + (column & 7)
    else:
        x, c, z = (column >> 4) & 3, (column >> 6) & 1, column & 15
    return x * 128 + z * 8 + c * 4 + k


def column_of(row):
    return ((row & 3) << 7) | (((row >> 2) & 1) << 6) | (row >> 3)


def reorder(values, received):
    n = len(values)
    row = iota((16, ROWS), 0)
    pieces = jnp.zeros((16, ROWS), F32)
    for i, value in enumerate(values):
        pieces = jnp.where(row == 2 * i, (value >> 6).astype(F32), pieces)
        pieces = jnp.where(row == 2 * i + 1, (value & 63).astype(F32), pieces)
    order = where_equal(iota((ROWS, ROWS), 0), natural(iota((ROWS, ROWS), 1), received))
    pieces = dot_nn(pieces.astype(BF16), order)
    return [pieces[2 * i : 2 * i + 1] * 64.0 + pieces[2 * i + 1 : 2 * i + 2] for i in range(n)]


def kernel(
    params,
    cam_in,
    send_rows_in,
    tiles_in,
    lists_in,
    counts_in,
    targets_in,
    gq,
    rendered,
    cam,
    send_rows,
    tiles,
    lists,
    counts,
    targets,
    lsem,
    pv,
    tail,
    pq,
    info,
    p3,
    oh,
    high,
    low,
    gs,
    fs,
    msg,
    mid,
    comp,
    got,
    ohr,
    ohs,
    names,
    upper,
    lower,
    fe,
    al,
    lk,
    bf,
    ws,
    sw2,
    rs,
    ge,
    psem,
    isend,
    irecv,
    zsend,
    zrecv,
    xsend,
    xrecv,
    near_sem,
    view_sem,
):
    me, my = lax.axis_index("gauss"), lax.axis_index("img")
    mx, mz, mc = me // 32, (me // 2) % 16, me % 2
    far_first = [8, 7, 9, 6, 10, 5, 11, 4, 12, 3, 13, 2, 14, 1, 15]
    z_peers = [(mz + j) % 16 for j in far_first]
    z_near = z_peers[7:]
    x_peers = [((mx + x) % 4, (mc + c) % 2) for x in (2, 1, 3, 0) for c in (0, 1)]
    x_others = x_peers[:6] + x_peers[7:]
    y_peers = [(my + y) % 4 for y in (2, 1, 3)]

    def tell(semaphore, device):
        pl.semaphore_signal(semaphore, inc=1, device_id=device, device_id_type=MESH)

    barrier = pltpu.get_barrier_semaphore()
    for z in z_near[:2]:
        tell(barrier, {"gauss": place(mx, z, mc)})
    for x, c in x_others:
        tell(barrier, {"gauss": place(x, mz, c)})
    for z in z_near[2:]:
        tell(barrier, {"gauss": place(mx, z, mc)})
    for y in y_peers:
        tell(barrier, {"img": y})

    loads = [
        pltpu.make_async_copy(source, target, lsem.at[n])
        for n, (source, target) in enumerate(
            [(send_rows_in, send_rows), (cam_in, cam), (lists_in, lists)]
            + [(tiles_in, tiles), (counts_in, counts), (targets_in, targets)]
        )
    ]
    loads[0].start()
    for part in range(4):
        columns = pl.ds(part * QUARTER, QUARTER)
        pltpu.make_async_copy(params.at[:, columns], pv.at[:, columns], psem).start()
    for copy in loads[1:]:
        copy.start()
    loads[0].wait()

    (chosen,) = reorder([send_rows[...]], False)

    @pl.loop(0, 64)
    def _(j):
        start = pl.multiple_of(j * 64, 64)
        gauss = (iota((64, ROWS), 0) + start).astype(F32)
        oh[pl.ds(start, 64), :] = where_equal(gauss, chosen)

    tail[...] = jnp.zeros((8, G_DEV), F32)
    pltpu.make_async_copy(params, pv, psem).wait()
    for copy in loads[1:]:
        copy.wait()

    @pl.loop(0, 16)
    def _(j):
        here = pl.ds(pl.multiple_of(j * 256, 256), 256)
        tail[0:3, here] = pv[56:PARAMS, here]
        whole = jnp.concatenate([pv[0:56, here], tail[:, here]], axis=0)
        for n, piece in enumerate(split(whole, 3)):
            p3[64 * n : 64 * (n + 1), here] = piece

    picked = dot_nn(p3[...], oh[...])
    gs[...] = picked[0:64] + picked[64:128] + picked[128:192]
    feats = project_rows([gs[f : f + 1, :] for f in range(PARAMS)], [cam[0, k] for k in range(16)])
    fs[8:16, :] = jnp.zeros((8, ROWS), F32)
    for f in range(FEATS):
        fs[f : f + 1, :] = feats[f]

    pl.semaphore_wait(barrier, 18)
    for z in z_near[:2]:
        tell(near_sem, {"gauss": place(mx, z, mc)})
    for y in y_peers:
        tell(view_sem, {"img": y})

    left = iota((8, 128), 1) < 64
    mine = mc * 4 + mx

    def halves(first, second):
        return jnp.where(left, first, pltpu.roll(second, 64, 1)), jnp.where(left, pltpu.roll(first, 64, 1), second)

    def send_z(turn):
        for z in z_peers:
            pltpu.make_async_remote_copy(
                src_ref=msg.at[turn, :, z], dst_ref=mid.at[turn, :, mz], send_sem=zsend.at[turn], recv_sem=zrecv.at[turn],
                device_id={"gauss": place(mx, z, mc)}, device_id_type=MESH,
            ).start()
        mid[turn, :, mz] = msg[turn, :, mz]

    def wait_z(turn, sems):
        span = mid.at[turn, :, pl.ds(0, 15)]
        pltpu.make_async_copy(span, span, sems.at[turn]).wait()

    def send_x(turn, x, c, y, slot):
        pltpu.make_async_remote_copy(
            src_ref=comp.at[turn, c * 4 + x], dst_ref=got.at[slot, mine], send_sem=xsend.at[turn],
            recv_sem=xrecv.at[slot], device_id={"gauss": place(x, mz, c), "img": y}, device_id_type=MESH,
        ).start()

    def wait_x(slot, count):
        span = got.at[slot, pl.ds(0, count)]
        pltpu.make_async_copy(span, span, xrecv.at[slot]).wait()

    def prepare():
        named = jnp.concatenate([lists[0, 0:1, :], lists[0, 1:2, :]], axis=1)
        named = column_of(named)
        names[...] = jnp.broadcast_to(named.astype(F32), (8, ROWS)).T

        @pl.loop(0, 8)
        def _(j):
            start = pl.multiple_of(j * 64, 64)
            ohr[pl.ds(start, 64), :] = where_equal(iota((64, ROWS), 0) + start, named)
            ohs[pl.ds(start, 64), :] = where_equal(iota((64, ROWS), 1).astype(F32), names[pl.ds(start, 64), 0:1])

        earlier = jnp.where(iota((LIST, LIST), 0) < iota((LIST, LIST), 1), 1.0, 0.0).astype(BF16)
        later = jnp.where(iota((LIST, LIST), 0) > iota((LIST, LIST), 1), 1.0, 0.0).astype(BF16)
        for n in range(2):
            upper[LIST * n : LIST * (n + 1), :] = earlier
            lower[LIST * n : LIST * (n + 1), :] = later
        rs[...] = jnp.zeros((2, 16, 256), F32)
        ge[8:16, :] = jnp.zeros((8, ROWS), F32)

    packed = as_message(fs[...])
    for x in range(4):
        comp[0, x], comp[0, 4 + x] = halves(packed[16 * x : 16 * x + 8], packed[16 * x + 8 : 16 * x + 16])
    for x, c in x_others:
        send_x(0, x, c, my, 4)
    got[4, mine] = comp[0, mine]
    for k in range(16):
        info[my, k : k + 1, :] = jnp.zeros((1, 128), F32) + cam[0, k]
    for k in range(4):
        info[my, 16 + k : 17 + k, :] = send_rows[:, k * 128 : (k + 1) * 128].astype(F32)
    info[my, 20:24, :] = jnp.zeros((4, 128), F32)
    for n, y in enumerate(y_peers):
        pltpu.make_async_remote_copy(
            src_ref=info.at[my], dst_ref=info.at[my], send_sem=isend.at[n], recv_sem=irecv.at[n],
            device_id={"img": y}, device_id_type=MESH,
        ).start()
    wait_x(4, 7)
    for x in range(4):
        low_z, high_z = halves(got[4, x], got[4, 4 + x])
        msg.reshape(128, 128)[16 * x : 16 * x + 8, :] = low_z
        msg.reshape(128, 128)[16 * x + 8 : 16 * x + 16, :] = high_z
    pl.semaphore_wait(near_sem, 2)
    send_z(0)
    prepare()
    wait_z(0, zrecv)
    received = as_columns(mid.reshape(128, 128)[0:64, :])

    listed = dot_nn(jnp.concatenate(split(received, 3), axis=0), ohr[...])
    fe[...] = listed[0:16] + listed[16:32] + listed[32:48]

    def entry(f, t):
        return fe[f : f + 1, t * LIST : (t + 1) * LIST]

    pixel = iota((16, LIST), 0).astype(F32)
    off_x, quad_x, cross, quad_y, origin_y, weight = [], [], [], [], [], []
    for t in range(2):
        tile = tiles[0, t]
        off_x.append(entry(0, t) - (pixel + ((tile & 15) * 16).astype(F32)))
        origin_y.append(entry(1, t) - ((tile >> 4) * 16).astype(F32))
        quad_x.append(-0.5 * entry(2, t) * off_x[t] * off_x[t])
        cross.append(-entry(3, t))
        quad_y.append(-0.5 * entry(4, t))
        weight.append(jnp.where(iota((1, LIST), 1) < counts[0, t], entry(8, t), 0.0))

    def pixels(t, j):
        return pl.ds(pl.multiple_of(t * 256 + j * 16, 16), 16)

    @pl.loop(0, 16, unroll=16)
    def _(j):
        for t in range(2):
            here = pixels(t, j)
            off_y = origin_y[t] - lax.convert_element_type(j, F32)
            power = quad_x[t] + off_x[t] * (cross[t] * off_y) + quad_y[t] * off_y * off_y
            alpha = weight[t] * jnp.exp(power)
            al[here, :] = alpha
            for n, piece in enumerate(split(jnp.log(1.0 - alpha), 2)):
                lk[here, LIST * n : LIST * (n + 1)] = piece

    bf[...] = dot_nn(lk[...], upper[...])

    @pl.loop(0, 16, unroll=16)
    def _(j):
        for t in range(2):
            here = pixels(t, j)
            ws[here, :] = al[here, :] * jnp.exp(bf[here, :])

    grad_colour = []
    for t in range(2):
        shown = split(ws[t * 256 : (t + 1) * 256, :], 3)
        tints = split(fe[:, t * LIST : (t + 1) * LIST], 3)
        stacked = jnp.concatenate(tints, axis=0)
        colours = dot_nt(stacked, shown[0]) + dot_nt(stacked, shown[1]) + dot_nt(stacked, shown[2])
        colours = (colours[0:16] + colours[16:32] + colours[32:48])[5:8]
        rendered[0, :, t, :] = colours
        rs[t, 5:8, :] = colours - targets[0, :, t, :]
        resid = split(rs[t], 2)
        stacked = jnp.concatenate(resid, axis=0)
        tinted = dot_nn(stacked, shown[0]) + dot_nn(stacked, shown[1])
        grad_colour.append(tinted[5:8] + tinted[21:24])
        resid = [piece.astype(F32) for piece in resid]
        turned = jnp.concatenate([resid[0], resid[1], resid[0]], axis=0).T.astype(BF16)
        bf[t * 256 : (t + 1) * 256, :] = dot_nn(turned, jnp.concatenate([tints[0], tints[0], tints[1]], axis=0))

    @pl.loop(0, 16, unroll=16)
    def _(j):
        for t in range(2):
            here = pixels(t, j)
            share = bf[here, :] * ws[here, :]
            ws[here, :] = share
            for n, piece in enumerate(split(share, 2)):
                sw2[here, LIST * n : LIST * (n + 1)] = piece

    bf[...] = dot_nn(sw2[...], lower[...])

    for t in range(2):

        def moments(j, carry):
            here = pixels(t, j)
            alpha = al[here, :]
            off_y = origin_y[t] - lax.convert_element_type(j, F32)
            flow = ws[here, :] - bf[here, :] * (alpha / (1.0 - alpha))
            flow_y = flow * off_y
            return carry[0] + flow, carry[1] + flow_y, carry[2] + flow_y * off_y

        zero = jnp.zeros((16, LIST), F32)
        flow, flow_y, flow_yy = lax.fori_loop(0, 16, moments, (zero, zero, zero), unroll=16)

        def over(value):
            return jnp.sum(value, axis=0, keepdims=True)

        m_x, m_y = over(flow * off_x[t]), over(flow_y)
        a, b, c = entry(2, t), entry(3, t), entry(4, t)
        out = [
            -(a * m_x + b * m_y),
            -(b * m_x + c * m_y),
            -0.5 * over(flow * off_x[t] * off_x[t]),
            -over(flow_y * off_x[t]),
            -0.5 * over(flow_yy),
            grad_colour[t][0:1],
            grad_colour[t][1:2],
            grad_colour[t][2:3],
            over(flow) / entry(8, t),
        ]
        for f in range(FEATS):
            ge[f : f + 1, t * LIST : (t + 1) * LIST] = out[f]

    back = dot_nn(jnp.concatenate(split(ge[...], 2), axis=0), ohs[...])
    msg.reshape(128, 128)[64:128, :] = as_message(back[0:16] + back[16:32])
    pulls = []

    def look_ahead():
        for n in range(3):
            pltpu.make_async_copy(info.at[0], info.at[0], irecv.at[n]).wait()
            pltpu.make_async_copy(info.at[0], info.at[0], isend.at[n]).wait()
        rows = [
            jnp.concatenate([info[view, 16 + k : 17 + k, :] for k in range(4)], axis=1).astype(jnp.int32)
            for view in range(4)
        ]
        for view, picks in enumerate(reorder(rows, True)):
            place_in = (picks - (my * QUARTER).astype(F32)).astype(jnp.int32)
            high[view] = jnp.where(iota((8, ROWS), 0) == (place_in >> 7), 1.0, 0.0)
            low[view] = jnp.where(iota((128, ROWS), 0) == (place_in & 127), 1.0, 0.0).T.astype(BF16)
        for block in range(8):
            pq[block] = pv[:, pl.ds(pl.multiple_of(my * QUARTER + block * 128, 128), 128)]
        own = [pq[:, f, :] for f in range(PARAMS)]
        for view in [my] + y_peers:
            camera = [jnp.broadcast_to(info[view, k : k + 1, :], (8, 128)) for k in range(16)]
            pulls.append(jax.vjp(lambda rows, camera=camera: project_rows(rows, camera), own)[1])

    send_z(1)
    look_ahead()
    wait_z(1, zrecv)
    for x in range(4):
        whole = mid.reshape(128, 128)[64 + 16 * x : 80 + 16 * x, :]
        comp[1, x], comp[1, 4 + x] = halves(whole[0:8], whole[8:16])
    pl.semaphore_wait(view_sem, 3)
    steps = [(x, c, y) for x in range(4) for c in range(2) for y in range(4) if (x, c, y) != (0, 0, 0)]
    steps.sort(key=lambda step: -min(step[0], 4 - step[0]) - min(step[2], 4 - step[2]))
    for x, c, y in steps:
        send_x(1, (mx + x) % 4, (mc + c) % 2, (my + y) % 4, my)
    got[my, mine] = comp[1, mine]
    for turn in range(2):
        wait_z(turn, zsend)

    def pulled(view, number):
        cols = as_columns(got[view].reshape(64, 128))
        parts = [high[view] * cols[f : f + 1] for f in range(FEATS)] + [jnp.zeros((8, ROWS), F32)]
        parts = split(jnp.concatenate(parts, axis=0), 2)
        sums = dot_nn(jnp.concatenate(parts, axis=0), low[view])
        sums = sums[0:80] + sums[80:160]
        (out,) = pulls[number]([sums[8 * f : 8 * f + 8] for f in range(FEATS)])
        return out

    wait_x(my, 7)
    total = pulled(my, 0)
    for y in y_peers:
        wait_x(y, 8)
    for n, y in ((1, y_peers[1]), (2, y_peers[2]), (0, y_peers[0])):
        total = [a + b for a, b in zip(total, pulled(y, n + 1))]
    for f in range(PARAMS):
        gq[:, f, :] = total[f]
    span = comp.at[0, pl.ds(0, 7)]
    pltpu.make_async_copy(span, span, xsend.at[0]).wait()
    span = got.at[0, pl.ds(0, 7)]
    pltpu.make_async_copy(span, span, xsend.at[1]).wait()
    span = got.at[pl.ds(0, 3)]
    pltpu.make_async_copy(span, span, xsend.at[1]).wait()


def finish(blocks, shown, grads, rendered, sem):
    copies = [pltpu.make_async_copy(blocks.at[b], grads.at[:, pl.ds(b * 128, 128)], sem.at[b]) for b in range(8)]
    copies.append(pltpu.make_async_copy(shown, rendered, sem.at[8]))
    for copy in copies:
        copy.start()
    for copy in copies:
        copy.wait()


def local(params, cameras, send_rows, tile_ids, lists, counts, targets):
    vmem, anywhere = (pl.BlockSpec(memory_space=s) for s in (pltpu.VMEM, pl.ANY))
    dma = pltpu.SemaphoreType.DMA
    operands = (params, cameras, send_rows, tile_ids, lists, counts, jnp.transpose(targets, (0, 2, 1, 3)))
    blocks, shown = pl.pallas_call(
        kernel,
        out_shape=(
            pltpu.VMEM((8, PARAMS, 128), F32),
            pltpu.VMEM((1, 3, 2, 256), F32),
        ),
        in_specs=[anywhere] * 7,
        out_specs=(vmem, vmem),
        scratch_shapes=[
            pltpu.SMEM((1, 16), F32),
            pltpu.VMEM((1, ROWS), jnp.int32),
            pltpu.SMEM((1, 2), jnp.int32),
            pltpu.VMEM((1, 2, LIST), jnp.int32),
            pltpu.SMEM((1, 2), jnp.int32),
            pltpu.VMEM((1, 3, 2, 256), F32),
            dma((6,)),
            pltpu.VMEM((PARAMS, G_DEV), F32),
            pltpu.VMEM((8, G_DEV), F32),
            pltpu.VMEM((8, PARAMS, 128), F32),
            pltpu.VMEM((4, 24, 128), F32),
            pltpu.VMEM((192, G_DEV), BF16),
            pltpu.VMEM((G_DEV, ROWS), BF16),
            pltpu.VMEM((4, 8, ROWS), F32),
            pltpu.VMEM((4, ROWS, 128), BF16),
            pltpu.VMEM((64, ROWS), F32),
            pltpu.VMEM((16, ROWS), F32),
            pltpu.VMEM((2, 4, 16, 1, 128), F32),
            pltpu.VMEM((2, 4, 16, 1, 128), F32),
            pltpu.VMEM((2, 8, 8, 128), F32),
            pltpu.VMEM((5, 8, 8, 128), F32),
            pltpu.VMEM((ROWS, ROWS), BF16),
            pltpu.VMEM((ROWS, ROWS), BF16),
            pltpu.VMEM((ROWS, 8), F32),
            pltpu.VMEM((2 * LIST, LIST), BF16),
            pltpu.VMEM((2 * LIST, LIST), BF16),
            pltpu.VMEM((16, ROWS), F32),
            pltpu.VMEM((512, LIST), F32),
            pltpu.VMEM((512, 2 * LIST), BF16),
            pltpu.VMEM((512, LIST), F32),
            pltpu.VMEM((512, LIST), F32),
            pltpu.VMEM((512, 2 * LIST), BF16),
            pltpu.VMEM((2, 16, 256), F32),
            pltpu.VMEM((16, ROWS), F32),
            dma,
            dma((3,)),
            dma((3,)),
            dma((2,)),
            dma((2,)),
            dma((2,)),
            dma((5,)),
            pltpu.SemaphoreType.REGULAR,
            pltpu.SemaphoreType.REGULAR,
        ],
        compiler_params=pltpu.CompilerParams(
            collective_id=0, has_side_effects=True, vmem_limit_bytes=32 * 1024 * 1024
        ),
    )(*(pltpu.with_memory_space_constraint(operand, pltpu.HBM) for operand in operands))
    grads, shown = pl.pallas_call(
        finish,
        out_shape=(
            jax.ShapeDtypeStruct((PARAMS, QUARTER), F32),
            jax.ShapeDtypeStruct((1, 3, 2, 256), F32),
        ),
        in_specs=[anywhere, anywhere],
        out_specs=(anywhere, anywhere),
        scratch_shapes=[dma((9,))],
    )(*(pltpu.with_memory_space_constraint(part, pltpu.VMEM) for part in (blocks, shown)))
    return grads, jnp.transpose(shown, (0, 2, 1, 3))


def solution(mesh):
    placed = (
        P(None, "gauss"),
        P("img", None),
        P("img", "gauss"),
        P("img", "gauss"),
        P("img", "gauss", None),
        P("img", "gauss"),
        P("img", "gauss", None, None),
    )
    return jax.shard_map(
        local,
        mesh=mesh,
        in_specs=placed,
        out_specs=(P(None, ("gauss", "img")), P("img", "gauss", None, None)),
        check_vma=False,
    )
```

```python
import jax
import jax.numpy as jnp
from jax import lax
from jax.experimental import pallas as pl
from jax.experimental.pallas import tpu as pltpu
from jax.sharding import PartitionSpec as P

MESH = pl.DeviceIdType.MESH
F32 = jnp.float32
BF16 = jnp.bfloat16
HIGHEST = lax.Precision.HIGHEST

FEATS = 9
PARAMS = 59
G_DEV = 4096
QUARTER = 1024
ROWS = 512
LIST = 256

sh_zero = 0.28209479177387814
sh_one = 0.4886025119029199
sh_two = [1.0925484305920792, -1.0925484305920792, 0.31539156525252005, -1.0925484305920792, 0.5462742152960396]
sh_three = [
    -0.5900435899266435,
    2.890611442640554,
    -0.4570457994644658,
    0.3731763325901154,
    -0.4570457994644658,
    1.445305721320277,
    -0.5900435899266435,
]


def project_rows(rows, camera):
    m = rows[0:3]
    rot = [[camera[3 * i + j] for j in range(3)] for i in range(3)]
    shift = camera[9:12]
    focal_x, focal_y, centre_x, centre_y = camera[12:16]
    p = [rot[i][0] * m[0] + rot[i][1] * m[1] + rot[i][2] * m[2] + shift[i] for i in range(3)]
    inv_z = 1.0 / p[2]
    xn, yn = p[0] * inv_z, p[1] * inv_z
    u = focal_x * xn + centre_x
    v = focal_y * yn + centre_y
    jx, jy = focal_x * inv_z, focal_y * inv_z
    q = rows[6:10]
    inv_q = 1.0 / jnp.sqrt(q[0] * q[0] + q[1] * q[1] + q[2] * q[2] + q[3] * q[3])
    w, x, y, z = (t * inv_q for t in q)
    rg = [
        [1.0 - 2.0 * (y * y + z * z), 2.0 * (x * y - w * z), 2.0 * (x * z + w * y)],
        [2.0 * (x * y + w * z), 1.0 - 2.0 * (x * x + z * z), 2.0 * (y * z - w * x)],
        [2.0 * (x * z - w * y), 2.0 * (y * z + w * x), 1.0 - 2.0 * (x * x + y * y)],
    ]
    scales = [jnp.exp(rows[3 + k]) for k in range(3)]
    sx = [jx * (rot[0][j] - xn * rot[2][j]) for j in range(3)]
    sy = [jy * (rot[1][j] - yn * rot[2][j]) for j in range(3)]
    bx = [(sx[0] * rg[0][k] + sx[1] * rg[1][k] + sx[2] * rg[2][k]) * scales[k] for k in range(3)]
    by = [(sy[0] * rg[0][k] + sy[1] * rg[1][k] + sy[2] * rg[2][k]) * scales[k] for k in range(3)]
    cxx = bx[0] * bx[0] + bx[1] * bx[1] + bx[2] * bx[2] + 0.3
    cxy = bx[0] * by[0] + bx[1] * by[1] + bx[2] * by[2]
    cyy = by[0] * by[0] + by[1] * by[1] + by[2] * by[2] + 0.3
    inv_det = 1.0 / (cxx * cyy - cxy * cxy)
    opacity = 1.0 / (1.0 + jnp.exp(-rows[10]))
    view = [m[j] + (rot[0][j] * shift[0] + rot[1][j] * shift[1] + rot[2][j] * shift[2]) for j in range(3)]
    inv_len = 1.0 / jnp.sqrt(view[0] * view[0] + view[1] * view[1] + view[2] * view[2])
    dx, dy, dz = (t * inv_len for t in view)
    xx, yy, zz = dx * dx, dy * dy, dz * dz
    basis = [
        -sh_one * dy,
        sh_one * dz,
        -sh_one * dx,
        sh_two[0] * dx * dy,
        sh_two[1] * dy * dz,
        sh_two[2] * (2.0 * zz - xx - yy),
        sh_two[3] * dx * dz,
        sh_two[4] * (xx - yy),
        sh_three[0] * dy * (3.0 * xx - yy),
        sh_three[1] * dx * dy * dz,
        sh_three[2] * dy * (4.0 * zz - xx - yy),
        sh_three[3] * dz * (2.0 * zz - 3.0 * xx - 3.0 * yy),
        sh_three[4] * dx * (4.0 * zz - xx - yy),
        sh_three[5] * dz * (xx - yy),
        sh_three[6] * dx * (xx - 3.0 * yy),
    ]
    colour = []
    for c in range(3):
        total = 0.5 + sh_zero * rows[11 + c]
        for k in range(1, 16):
            total = total + basis[k - 1] * rows[11 + 3 * k + c]
        colour.append(total)
    return [u, v, cyy * inv_det, -cxy * inv_det, cxx * inv_det, *colour, opacity]


def split(value, parts):
    out = []
    for _ in range(parts - 1):
        piece = value.astype(BF16)
        out.append(piece)
        value = value - piece.astype(F32)
    out.append(value.astype(BF16))
    return out


def dot_nn(a, b, precision=None):
    return lax.dot_general(a, b, (((1,), (0,)), ((), ())), precision=precision, preferred_element_type=F32)


def dot_nt(a, b, precision=None):
    return lax.dot_general(a, b, (((1,), (1,)), ((), ())), precision=precision, preferred_element_type=F32)


def where_equal(a, b):
    return jnp.where(a == b, 1.0, 0.0).astype(BF16)


def iota(shape, dim):
    return lax.broadcasted_iota(jnp.int32, shape, dim)


def place(x, z, c):
    return (x * 16 + z) * 2 + c


def as_message(feats):
    blocks = [feats[:, k * 128 : (k + 1) * 128] for k in range(4)]
    both = jnp.concatenate(blocks + blocks, axis=0).T
    return jnp.where(iota((64, 128), 1) < 64, both[0:64], both[64:128])


def as_columns(rows):
    both = jnp.concatenate([rows, rows], axis=0).T
    left = iota((16, 128), 1) < 64
    blocks = [jnp.where(left, both[16 * k : 16 * k + 16], both[64 + 16 * k : 80 + 16 * k]) for k in range(4)]
    return jnp.concatenate(blocks, axis=1)


def natural(column, received):
    k = column >> 7
    if received:
        x, c = (column >> 3) & 3, (column >> 5) & 1
        z = ((column >> 6) & 1) * 8 + (column & 7)
    else:
        x, c, z = (column >> 4) & 3, (column >> 6) & 1, column & 15
    return x * 128 + z * 8 + c * 4 + k


def column_of(row):
    return ((row & 3) << 7) | (((row >> 2) & 1) << 6) | (row >> 3)


def reorder(values, received):
    n = len(values)
    row = iota((16, ROWS), 0)
    pieces = jnp.zeros((16, ROWS), F32)
    for i, value in enumerate(values):
        pieces = jnp.where(row == 2 * i, (value >> 6).astype(F32), pieces)
        pieces = jnp.where(row == 2 * i + 1, (value & 63).astype(F32), pieces)
    order = where_equal(iota((ROWS, ROWS), 0), natural(iota((ROWS, ROWS), 1), received))
    pieces = dot_nn(pieces.astype(BF16), order)
    return [pieces[2 * i : 2 * i + 1] * 64.0 + pieces[2 * i + 1 : 2 * i + 2] for i in range(n)]


def kernel(
    params,
    cam_in,
    send_rows_in,
    tiles_in,
    lists_in,
    counts_in,
    targets_in,
    gq,
    rendered,
    cam,
    send_rows,
    tiles,
    lists,
    counts,
    targets,
    lsem,
    pv,
    tail,
    pq,
    info,
    p3,
    oh,
    high,
    low,
    gs,
    fs,
    msg,
    mid,
    comp,
    got,
    ohr,
    ohs,
    names,
    upper,
    lower,
    fe,
    al,
    lk,
    bf,
    ws,
    sw2,
    rs,
    ge,
    psem,
    isend,
    irecv,
    zsend,
    zrecv,
    xsend,
    xrecv,
    near_sem,
    view_sem,
):
    me, my = lax.axis_index("gauss"), lax.axis_index("img")
    mx, mz, mc = me // 32, (me // 2) % 16, me % 2
    far_first = [8, 7, 9, 6, 10, 5, 11, 4, 12, 3, 13, 2, 14, 1, 15]
    z_peers = [(mz + j) % 16 for j in far_first]
    z_near = z_peers[7:]
    x_peers = [((mx + x) % 4, (mc + c) % 2) for x in (2, 1, 3, 0) for c in (0, 1)]
    x_others = x_peers[:6] + x_peers[7:]
    y_peers = [(my + y) % 4 for y in (2, 1, 3)]

    def tell(semaphore, device):
        pl.semaphore_signal(semaphore, inc=1, device_id=device, device_id_type=MESH)

    barrier = pltpu.get_barrier_semaphore()
    for z in z_near[:2]:
        tell(barrier, {"gauss": place(mx, z, mc)})
    for x, c in x_others:
        tell(barrier, {"gauss": place(x, mz, c)})
    for z in z_near[2:]:
        tell(barrier, {"gauss": place(mx, z, mc)})
    for y in y_peers:
        tell(barrier, {"img": y})

    loads = [
        pltpu.make_async_copy(source, target, lsem.at[n])
        for n, (source, target) in enumerate(
            [(send_rows_in, send_rows), (cam_in, cam), (lists_in, lists)]
            + [(tiles_in, tiles), (counts_in, counts), (targets_in, targets)]
        )
    ]
    loads[0].start()
    for part in range(4):
        columns = pl.ds(part * QUARTER, QUARTER)
        pltpu.make_async_copy(params.at[:, columns], pv.at[:, columns], psem).start()
    for copy in loads[1:]:
        copy.start()
    loads[0].wait()

    (chosen,) = reorder([send_rows[...]], False)

    @pl.loop(0, 64)
    def _(j):
        start = pl.multiple_of(j * 64, 64)
        gauss = (iota((64, ROWS), 0) + start).astype(F32)
        oh[pl.ds(start, 64), :] = where_equal(gauss, chosen)

    tail[...] = jnp.zeros((8, G_DEV), F32)
    pltpu.make_async_copy(params, pv, psem).wait()
    for copy in loads[1:]:
        copy.wait()

    @pl.loop(0, 16)
    def _(j):
        here = pl.ds(pl.multiple_of(j * 256, 256), 256)
        tail[0:3, here] = pv[56:PARAMS, here]
        whole = jnp.concatenate([pv[0:56, here], tail[:, here]], axis=0)
        for n, piece in enumerate(split(whole, 3)):
            p3[64 * n : 64 * (n + 1), here] = piece

    picked = dot_nn(p3[...], oh[...])
    gs[...] = picked[0:64] + picked[64:128] + picked[128:192]
    feats = project_rows([gs[f : f + 1, :] for f in range(PARAMS)], [cam[0, k] for k in range(16)])
    fs[8:16, :] = jnp.zeros((8, ROWS), F32)
    for f in range(FEATS):
        fs[f : f + 1, :] = feats[f]
    left = iota((8, 128), 1) < 64
    mine = mc * 4 + mx

    def halves(first, second):
        return jnp.where(left, first, pltpu.roll(second, 64, 1)), jnp.where(left, pltpu.roll(first, 64, 1), second)

    packed = as_message(fs[...])
    for x in range(4):
        comp[0, x], comp[0, 4 + x] = halves(packed[16 * x : 16 * x + 8], packed[16 * x + 8 : 16 * x + 16])
    got[4, mine] = comp[0, mine]

    pl.semaphore_wait(barrier, 18)
    for z in z_near[:2]:
        tell(near_sem, {"gauss": place(mx, z, mc)})

    def send_z(turn):
        for z in z_peers:
            pltpu.make_async_remote_copy(
                src_ref=msg.at[turn, :, z], dst_ref=mid.at[turn, :, mz], send_sem=zsend.at[turn], recv_sem=zrecv.at[turn],
                device_id={"gauss": place(mx, z, mc)}, device_id_type=MESH,
            ).start()
        mid[turn, :, mz] = msg[turn, :, mz]

    def wait_z(turn, sems):
        span = mid.at[turn, :, pl.ds(0, 15)]
        pltpu.make_async_copy(span, span, sems.at[turn]).wait()

    def send_x(turn, x, c, y, slot):
        pltpu.make_async_remote_copy(
            src_ref=comp.at[turn, c * 4 + x], dst_ref=got.at[slot, mine], send_sem=xsend.at[turn],
            recv_sem=xrecv.at[slot], device_id={"gauss": place(x, mz, c), "img": y}, device_id_type=MESH,
        ).start()

    def wait_x(slot, count):
        span = got.at[slot, pl.ds(0, count)]
        pltpu.make_async_copy(span, span, xrecv.at[slot]).wait()

    def prepare():
        named = jnp.concatenate([lists[0, 0:1, :], lists[0, 1:2, :]], axis=1)
        named = column_of(named)
        names[...] = jnp.broadcast_to(named.astype(F32), (8, ROWS)).T

        @pl.loop(0, 8)
        def _(j):
            start = pl.multiple_of(j * 64, 64)
            ohr[pl.ds(start, 64), :] = where_equal(iota((64, ROWS), 0) + start, named)
            ohs[pl.ds(start, 64), :] = where_equal(iota((64, ROWS), 1).astype(F32), names[pl.ds(start, 64), 0:1])

        earlier = jnp.where(iota((LIST, LIST), 0) < iota((LIST, LIST), 1), 1.0, 0.0).astype(BF16)
        later = jnp.where(iota((LIST, LIST), 0) > iota((LIST, LIST), 1), 1.0, 0.0).astype(BF16)
        for n in range(2):
            upper[LIST * n : LIST * (n + 1), :] = earlier
            lower[LIST * n : LIST * (n + 1), :] = later
        rs[...] = jnp.zeros((2, 16, 256), F32)
        ge[8:16, :] = jnp.zeros((8, ROWS), F32)

    for x, c in x_others:
        send_x(0, x, c, my, 4)
    for y in y_peers:
        tell(view_sem, {"img": y})
    for k in range(16):
        info[my, k : k + 1, :] = jnp.zeros((1, 128), F32) + cam[0, k]
    for k in range(4):
        info[my, 16 + k : 17 + k, :] = send_rows[:, k * 128 : (k + 1) * 128].astype(F32)
    info[my, 20:24, :] = jnp.zeros((4, 128), F32)
    wait_x(4, 7)
    for x in range(4):
        low_z, high_z = halves(got[4, x], got[4, 4 + x])
        msg.reshape(128, 128)[16 * x : 16 * x + 8, :] = low_z
        msg.reshape(128, 128)[16 * x + 8 : 16 * x + 16, :] = high_z
    pl.semaphore_wait(near_sem, 2)
    send_z(0)
    for n, y in enumerate(y_peers):
        pltpu.make_async_remote_copy(
            src_ref=info.at[my], dst_ref=info.at[my], send_sem=isend.at[n], recv_sem=irecv.at[n],
            device_id={"img": y}, device_id_type=MESH,
        ).start()
    prepare()
    wait_z(0, zrecv)
    received = as_columns(mid.reshape(128, 128)[0:64, :])

    listed = dot_nn(jnp.concatenate(split(received, 3), axis=0), ohr[...])
    fe[...] = listed[0:16] + listed[16:32] + listed[32:48]

    def entry(f, t):
        return fe[f : f + 1, t * LIST : (t + 1) * LIST]

    pixel = iota((16, LIST), 0).astype(F32)
    off_x, quad_x, cross, quad_y, origin_y, weight = [], [], [], [], [], []
    for t in range(2):
        tile = tiles[0, t]
        off_x.append(entry(0, t) - (pixel + ((tile & 15) * 16).astype(F32)))
        origin_y.append(entry(1, t) - ((tile >> 4) * 16).astype(F32))
        quad_x.append(-0.5 * entry(2, t) * off_x[t] * off_x[t])
        cross.append(-entry(3, t))
        quad_y.append(-0.5 * entry(4, t))
        weight.append(jnp.where(iota((1, LIST), 1) < counts[0, t], entry(8, t), 0.0))

    def pixels(t, j):
        return pl.ds(pl.multiple_of(t * 256 + j * 16, 16), 16)

    @pl.loop(0, 16, unroll=16)
    def _(j):
        for t in range(2):
            here = pixels(t, j)
            off_y = origin_y[t] - lax.convert_element_type(j, F32)
            power = quad_x[t] + off_x[t] * (cross[t] * off_y) + quad_y[t] * off_y * off_y
            alpha = weight[t] * jnp.exp(power)
            al[here, :] = alpha
            for n, piece in enumerate(split(jnp.log(1.0 - alpha), 2)):
                lk[here, LIST * n : LIST * (n + 1)] = piece

    bf[...] = dot_nn(lk[...], upper[...])

    @pl.loop(0, 16, unroll=16)
    def _(j):
        for t in range(2):
            here = pixels(t, j)
            ws[here, :] = al[here, :] * jnp.exp(bf[here, :])

    grad_colour = []
    for t in range(2):
        shown = split(ws[t * 256 : (t + 1) * 256, :], 3)
        tints = split(fe[:, t * LIST : (t + 1) * LIST], 3)
        stacked = jnp.concatenate(tints, axis=0)
        colours = dot_nt(stacked, shown[0]) + dot_nt(stacked, shown[1]) + dot_nt(stacked, shown[2])
        colours = (colours[0:16] + colours[16:32] + colours[32:48])[5:8]
        rendered[0, :, t, :] = colours
        rs[t, 5:8, :] = colours - targets[0, :, t, :]
        resid = split(rs[t], 2)
        stacked = jnp.concatenate(resid, axis=0)
        tinted = dot_nn(stacked, shown[0]) + dot_nn(stacked, shown[1])
        grad_colour.append(tinted[5:8] + tinted[21:24])
        resid = [piece.astype(F32) for piece in resid]
        turned = jnp.concatenate([resid[0], resid[1], resid[0]], axis=0).T.astype(BF16)
        bf[t * 256 : (t + 1) * 256, :] = dot_nn(turned, jnp.concatenate([tints[0], tints[0], tints[1]], axis=0))

    @pl.loop(0, 16, unroll=16)
    def _(j):
        for t in range(2):
            here = pixels(t, j)
            share = bf[here, :] * ws[here, :]
            ws[here, :] = share
            for n, piece in enumerate(split(share, 2)):
                sw2[here, LIST * n : LIST * (n + 1)] = piece

    bf[...] = dot_nn(sw2[...], lower[...])

    for t in range(2):

        def moments(j, carry):
            here = pixels(t, j)
            alpha = al[here, :]
            off_y = origin_y[t] - lax.convert_element_type(j, F32)
            flow = ws[here, :] - bf[here, :] * (alpha / (1.0 - alpha))
            flow_y = flow * off_y
            return carry[0] + flow, carry[1] + flow_y, carry[2] + flow_y * off_y

        zero = jnp.zeros((16, LIST), F32)
        flow, flow_y, flow_yy = lax.fori_loop(0, 16, moments, (zero, zero, zero), unroll=16)

        def over(value):
            return jnp.sum(value, axis=0, keepdims=True)

        m_x, m_y = over(flow * off_x[t]), over(flow_y)
        a, b, c = entry(2, t), entry(3, t), entry(4, t)
        out = [
            -(a * m_x + b * m_y),
            -(b * m_x + c * m_y),
            -0.5 * over(flow * off_x[t] * off_x[t]),
            -over(flow_y * off_x[t]),
            -0.5 * over(flow_yy),
            grad_colour[t][0:1],
            grad_colour[t][1:2],
            grad_colour[t][2:3],
            over(flow) / entry(8, t),
        ]
        for f in range(FEATS):
            ge[f : f + 1, t * LIST : (t + 1) * LIST] = out[f]

    back = dot_nn(jnp.concatenate(split(ge[...], 2), axis=0), ohs[...])
    msg.reshape(128, 128)[64:128, :] = as_message(back[0:16] + back[16:32])
    pulls = []

    def look_ahead():
        for n in range(3):
            pltpu.make_async_copy(info.at[0], info.at[0], irecv.at[n]).wait()
            pltpu.make_async_copy(info.at[0], info.at[0], isend.at[n]).wait()
        rows = [
            jnp.concatenate([info[view, 16 + k : 17 + k, :] for k in range(4)], axis=1).astype(jnp.int32)
            for view in range(4)
        ]
        for view, picks in enumerate(reorder(rows, True)):
            place_in = (picks - (my * QUARTER).astype(F32)).astype(jnp.int32)
            high[view] = jnp.where(iota((8, ROWS), 0) == (place_in >> 7), 1.0, 0.0)
            low[view] = jnp.where(iota((128, ROWS), 0) == (place_in & 127), 1.0, 0.0).T.astype(BF16)
        for block in range(8):
            pq[block] = pv[:, pl.ds(pl.multiple_of(my * QUARTER + block * 128, 128), 128)]
        own = [pq[:, f, :] for f in range(PARAMS)]
        for view in [my] + y_peers:
            camera = [jnp.broadcast_to(info[view, k : k + 1, :], (8, 128)) for k in range(16)]
            pulls.append(jax.vjp(lambda rows, camera=camera: project_rows(rows, camera), own)[1])

    send_z(1)
    look_ahead()
    wait_z(1, zrecv)
    for x in range(4):
        whole = mid.reshape(128, 128)[64 + 16 * x : 80 + 16 * x, :]
        comp[1, x], comp[1, 4 + x] = halves(whole[0:8], whole[8:16])
    pl.semaphore_wait(view_sem, 3)
    steps = [(x, c, y) for x in range(4) for c in range(2) for y in range(4) if (x, c, y) != (0, 0, 0)]
    steps.sort(key=lambda step: -min(step[0], 4 - step[0]) - min(step[2], 4 - step[2]))
    for x, c, y in steps:
        send_x(1, (mx + x) % 4, (mc + c) % 2, (my + y) % 4, my)
    got[my, mine] = comp[1, mine]
    for turn in range(2):
        wait_z(turn, zsend)

    def pulled(view, number):
        cols = as_columns(got[view].reshape(64, 128))
        parts = [high[view] * cols[f : f + 1] for f in range(FEATS)] + [jnp.zeros((8, ROWS), F32)]
        parts = split(jnp.concatenate(parts, axis=0), 2)
        sums = dot_nn(jnp.concatenate(parts, axis=0), low[view])
        sums = sums[0:80] + sums[80:160]
        (out,) = pulls[number]([sums[8 * f : 8 * f + 8] for f in range(FEATS)])
        return out

    wait_x(my, 7)
    total = pulled(my, 0)
    for y in y_peers:
        wait_x(y, 8)
    for n, y in ((1, y_peers[1]), (2, y_peers[2]), (0, y_peers[0])):
        total = [a + b for a, b in zip(total, pulled(y, n + 1))]
    for f in range(PARAMS):
        gq[:, f, :] = total[f]
    span = comp.at[0, pl.ds(0, 7)]
    pltpu.make_async_copy(span, span, xsend.at[0]).wait()
    span = got.at[0, pl.ds(0, 7)]
    pltpu.make_async_copy(span, span, xsend.at[1]).wait()
    span = got.at[pl.ds(0, 3)]
    pltpu.make_async_copy(span, span, xsend.at[1]).wait()


def finish(blocks, shown, grads, rendered, sem):
    copies = [pltpu.make_async_copy(blocks.at[b], grads.at[:, pl.ds(b * 128, 128)], sem.at[b]) for b in range(8)]
    copies.append(pltpu.make_async_copy(shown, rendered, sem.at[8]))
    for copy in copies:
        copy.start()
    for copy in copies:
        copy.wait()


def local(params, cameras, send_rows, tile_ids, lists, counts, targets):
    vmem, anywhere = (pl.BlockSpec(memory_space=s) for s in (pltpu.VMEM, pl.ANY))
    dma = pltpu.SemaphoreType.DMA
    operands = (params, cameras, send_rows, tile_ids, lists, counts, jnp.transpose(targets, (0, 2, 1, 3)))
    blocks, shown = pl.pallas_call(
        kernel,
        out_shape=(
            pltpu.VMEM((8, PARAMS, 128), F32),
            pltpu.VMEM((1, 3, 2, 256), F32),
        ),
        in_specs=[anywhere] * 7,
        out_specs=(vmem, vmem),
        scratch_shapes=[
            pltpu.SMEM((1, 16), F32),
            pltpu.VMEM((1, ROWS), jnp.int32),
            pltpu.SMEM((1, 2), jnp.int32),
            pltpu.VMEM((1, 2, LIST), jnp.int32),
            pltpu.SMEM((1, 2), jnp.int32),
            pltpu.VMEM((1, 3, 2, 256), F32),
            dma((6,)),
            pltpu.VMEM((PARAMS, G_DEV), F32),
            pltpu.VMEM((8, G_DEV), F32),
            pltpu.VMEM((8, PARAMS, 128), F32),
            pltpu.VMEM((4, 24, 128), F32),
            pltpu.VMEM((192, G_DEV), BF16),
            pltpu.VMEM((G_DEV, ROWS), BF16),
            pltpu.VMEM((4, 8, ROWS), F32),
            pltpu.VMEM((4, ROWS, 128), BF16),
            pltpu.VMEM((64, ROWS), F32),
            pltpu.VMEM((16, ROWS), F32),
            pltpu.VMEM((2, 4, 16, 1, 128), F32),
            pltpu.VMEM((2, 4, 16, 1, 128), F32),
            pltpu.VMEM((2, 8, 8, 128), F32),
            pltpu.VMEM((5, 8, 8, 128), F32),
            pltpu.VMEM((ROWS, ROWS), BF16),
            pltpu.VMEM((ROWS, ROWS), BF16),
            pltpu.VMEM((ROWS, 8), F32),
            pltpu.VMEM((2 * LIST, LIST), BF16),
            pltpu.VMEM((2 * LIST, LIST), BF16),
            pltpu.VMEM((16, ROWS), F32),
            pltpu.VMEM((512, LIST), F32),
            pltpu.VMEM((512, 2 * LIST), BF16),
            pltpu.VMEM((512, LIST), F32),
            pltpu.VMEM((512, LIST), F32),
            pltpu.VMEM((512, 2 * LIST), BF16),
            pltpu.VMEM((2, 16, 256), F32),
            pltpu.VMEM((16, ROWS), F32),
            dma,
            dma((3,)),
            dma((3,)),
            dma((2,)),
            dma((2,)),
            dma((2,)),
            dma((5,)),
            pltpu.SemaphoreType.REGULAR,
            pltpu.SemaphoreType.REGULAR,
        ],
        compiler_params=pltpu.CompilerParams(
            collective_id=0, has_side_effects=True, vmem_limit_bytes=32 * 1024 * 1024
        ),
    )(*(pltpu.with_memory_space_constraint(operand, pltpu.HBM) for operand in operands))
    grads, shown = pl.pallas_call(
        finish,
        out_shape=(
            jax.ShapeDtypeStruct((PARAMS, QUARTER), F32),
            jax.ShapeDtypeStruct((1, 3, 2, 256), F32),
        ),
        in_specs=[anywhere, anywhere],
        out_specs=(anywhere, anywhere),
        scratch_shapes=[dma((9,))],
    )(*(pltpu.with_memory_space_constraint(part, pltpu.VMEM) for part in (blocks, shown)))
    return grads, jnp.transpose(shown, (0, 2, 1, 3))


def solution(mesh):
    placed = (
        P(None, "gauss"),
        P("img", None),
        P("img", "gauss"),
        P("img", "gauss"),
        P("img", "gauss", None),
        P("img", "gauss"),
        P("img", "gauss", None, None),
    )
    return jax.shard_map(
        local,
        mesh=mesh,
        in_specs=placed,
        out_specs=(P(None, ("gauss", "img")), P("img", "gauss", None, None)),
        check_vma=False,
    )
```

```python
import jax
import jax.numpy as jnp
from jax import lax
from jax.experimental import pallas as pl
from jax.experimental.pallas import tpu as pltpu
from jax.sharding import PartitionSpec as P

MESH = pl.DeviceIdType.MESH
F32 = jnp.float32
BF16 = jnp.bfloat16
HIGHEST = lax.Precision.HIGHEST

FEATS = 9
PARAMS = 59
G_DEV = 4096
QUARTER = 1024
ROWS = 512
LIST = 256

sh_zero = 0.28209479177387814
sh_one = 0.4886025119029199
sh_two = [1.0925484305920792, -1.0925484305920792, 0.31539156525252005, -1.0925484305920792, 0.5462742152960396]
sh_three = [
    -0.5900435899266435,
    2.890611442640554,
    -0.4570457994644658,
    0.3731763325901154,
    -0.4570457994644658,
    1.445305721320277,
    -0.5900435899266435,
]


def project_rows(rows, camera):
    m = rows[0:3]
    rot = [[camera[3 * i + j] for j in range(3)] for i in range(3)]
    shift = camera[9:12]
    focal_x, focal_y, centre_x, centre_y = camera[12:16]
    p = [rot[i][0] * m[0] + rot[i][1] * m[1] + rot[i][2] * m[2] + shift[i] for i in range(3)]
    inv_z = 1.0 / p[2]
    xn, yn = p[0] * inv_z, p[1] * inv_z
    u = focal_x * xn + centre_x
    v = focal_y * yn + centre_y
    jx, jy = focal_x * inv_z, focal_y * inv_z
    q = rows[6:10]
    inv_q = 1.0 / jnp.sqrt(q[0] * q[0] + q[1] * q[1] + q[2] * q[2] + q[3] * q[3])
    w, x, y, z = (t * inv_q for t in q)
    rg = [
        [1.0 - 2.0 * (y * y + z * z), 2.0 * (x * y - w * z), 2.0 * (x * z + w * y)],
        [2.0 * (x * y + w * z), 1.0 - 2.0 * (x * x + z * z), 2.0 * (y * z - w * x)],
        [2.0 * (x * z - w * y), 2.0 * (y * z + w * x), 1.0 - 2.0 * (x * x + y * y)],
    ]
    scales = [jnp.exp(rows[3 + k]) for k in range(3)]
    sx = [jx * (rot[0][j] - xn * rot[2][j]) for j in range(3)]
    sy = [jy * (rot[1][j] - yn * rot[2][j]) for j in range(3)]
    bx = [(sx[0] * rg[0][k] + sx[1] * rg[1][k] + sx[2] * rg[2][k]) * scales[k] for k in range(3)]
    by = [(sy[0] * rg[0][k] + sy[1] * rg[1][k] + sy[2] * rg[2][k]) * scales[k] for k in range(3)]
    cxx = bx[0] * bx[0] + bx[1] * bx[1] + bx[2] * bx[2] + 0.3
    cxy = bx[0] * by[0] + bx[1] * by[1] + bx[2] * by[2]
    cyy = by[0] * by[0] + by[1] * by[1] + by[2] * by[2] + 0.3
    inv_det = 1.0 / (cxx * cyy - cxy * cxy)
    opacity = 1.0 / (1.0 + jnp.exp(-rows[10]))
    view = [m[j] + (rot[0][j] * shift[0] + rot[1][j] * shift[1] + rot[2][j] * shift[2]) for j in range(3)]
    inv_len = 1.0 / jnp.sqrt(view[0] * view[0] + view[1] * view[1] + view[2] * view[2])
    dx, dy, dz = (t * inv_len for t in view)
    xx, yy, zz = dx * dx, dy * dy, dz * dz
    basis = [
        -sh_one * dy,
        sh_one * dz,
        -sh_one * dx,
        sh_two[0] * dx * dy,
        sh_two[1] * dy * dz,
        sh_two[2] * (2.0 * zz - xx - yy),
        sh_two[3] * dx * dz,
        sh_two[4] * (xx - yy),
        sh_three[0] * dy * (3.0 * xx - yy),
        sh_three[1] * dx * dy * dz,
        sh_three[2] * dy * (4.0 * zz - xx - yy),
        sh_three[3] * dz * (2.0 * zz - 3.0 * xx - 3.0 * yy),
        sh_three[4] * dx * (4.0 * zz - xx - yy),
        sh_three[5] * dz * (xx - yy),
        sh_three[6] * dx * (xx - 3.0 * yy),
    ]
    colour = []
    for c in range(3):
        total = 0.5 + sh_zero * rows[11 + c]
        for k in range(1, 16):
            total = total + basis[k - 1] * rows[11 + 3 * k + c]
        colour.append(total)
    return [u, v, cyy * inv_det, -cxy * inv_det, cxx * inv_det, *colour, opacity]


def split(value, parts):
    out = []
    for _ in range(parts - 1):
        piece = value.astype(BF16)
        out.append(piece)
        value = value - piece.astype(F32)
    out.append(value.astype(BF16))
    return out


def dot_nn(a, b, precision=None):
    return lax.dot_general(a, b, (((1,), (0,)), ((), ())), precision=precision, preferred_element_type=F32)


def dot_nt(a, b, precision=None):
    return lax.dot_general(a, b, (((1,), (1,)), ((), ())), precision=precision, preferred_element_type=F32)


def where_equal(a, b):
    return jnp.where(a == b, 1.0, 0.0).astype(BF16)


def iota(shape, dim):
    return lax.broadcasted_iota(jnp.int32, shape, dim)


def place(x, z, c):
    return (x * 16 + z) * 2 + c


def as_message(feats):
    blocks = [feats[:, k * 128 : (k + 1) * 128] for k in range(4)]
    both = jnp.concatenate(blocks + blocks, axis=0).T
    return jnp.where(iota((64, 128), 1) < 64, both[0:64], both[64:128])


def as_columns(rows):
    both = jnp.concatenate([rows, rows], axis=0).T
    left = iota((16, 128), 1) < 64
    blocks = [jnp.where(left, both[16 * k : 16 * k + 16], both[64 + 16 * k : 80 + 16 * k]) for k in range(4)]
    return jnp.concatenate(blocks, axis=1)


def natural(column, received):
    k = column >> 7
    if received:
        x, c = (column >> 3) & 3, (column >> 5) & 1
        z = ((column >> 6) & 1) * 8 + (column & 7)
    else:
        x, c, z = (column >> 4) & 3, (column >> 6) & 1, column & 15
    return x * 128 + z * 8 + c * 4 + k


def column_of(row):
    return ((row & 3) << 7) | (((row >> 2) & 1) << 6) | (row >> 3)


def reorder(values, received):
    n = len(values)
    row = iota((16, ROWS), 0)
    pieces = jnp.zeros((16, ROWS), F32)
    for i, value in enumerate(values):
        pieces = jnp.where(row == 2 * i, (value >> 6).astype(F32), pieces)
        pieces = jnp.where(row == 2 * i + 1, (value & 63).astype(F32), pieces)
    order = where_equal(iota((ROWS, ROWS), 0), natural(iota((ROWS, ROWS), 1), received))
    pieces = dot_nn(pieces.astype(BF16), order)
    return [pieces[2 * i : 2 * i + 1] * 64.0 + pieces[2 * i + 1 : 2 * i + 2] for i in range(n)]


def kernel(
    params,
    cam_in,
    send_rows_in,
    tiles_in,
    lists_in,
    counts_in,
    targets_in,
    gq,
    rendered,
    cam,
    send_rows,
    tiles,
    lists,
    counts,
    targets,
    lsem,
    pv,
    tail,
    pq,
    info,
    p3,
    oh,
    high,
    low,
    gs,
    fs,
    msg,
    mid,
    comp,
    got,
    ohr,
    ohs,
    names,
    upper,
    lower,
    fe,
    al,
    lk,
    bf,
    ws,
    sw2,
    rs,
    ge,
    psem,
    isend,
    irecv,
    zsend,
    zrecv,
    xsend,
    xrecv,
    near_sem,
    view_sem,
):
    me, my = lax.axis_index("gauss"), lax.axis_index("img")
    mx, mz, mc = me // 32, (me // 2) % 16, me % 2
    far_first = [8, 7, 9, 6, 10, 5, 11, 4, 12, 3, 13, 2, 14, 1, 15]
    z_peers = [(mz + j) % 16 for j in far_first]
    z_near = z_peers[7:]
    x_peers = [((mx + x) % 4, (mc + c) % 2) for x in (2, 1, 3, 0) for c in (0, 1)]
    x_others = x_peers[:6] + x_peers[7:]
    y_peers = [(my + y) % 4 for y in (2, 1, 3)]

    def tell(semaphore, device):
        pl.semaphore_signal(semaphore, inc=1, device_id=device, device_id_type=MESH)

    barrier = pltpu.get_barrier_semaphore()
    for z in z_near[:2]:
        tell(barrier, {"gauss": place(mx, z, mc)})
    for x, c in x_others:
        tell(barrier, {"gauss": place(x, mz, c)})
    for z in z_near[2:]:
        tell(barrier, {"gauss": place(mx, z, mc)})
    for y in y_peers:
        tell(barrier, {"img": y})

    loads = [
        pltpu.make_async_copy(source, target, lsem.at[n])
        for n, (source, target) in enumerate(
            [(send_rows_in, send_rows), (cam_in, cam), (lists_in, lists)]
            + [(tiles_in, tiles), (counts_in, counts), (targets_in, targets)]
        )
    ]
    loads[0].start()
    for part in range(4):
        columns = pl.ds(part * QUARTER, QUARTER)
        pltpu.make_async_copy(params.at[:, columns], pv.at[:, columns], psem).start()
    for copy in loads[1:]:
        copy.start()
    loads[0].wait()

    (chosen,) = reorder([send_rows[...]], False)

    @pl.loop(0, 64)
    def _(j):
        start = pl.multiple_of(j * 64, 64)
        gauss = (iota((64, ROWS), 0) + start).astype(F32)
        oh[pl.ds(start, 64), :] = where_equal(gauss, chosen)

    tail[...] = jnp.zeros((8, G_DEV), F32)
    pltpu.make_async_copy(params, pv, psem).wait()
    for copy in loads[1:]:
        copy.wait()

    @pl.loop(0, 16)
    def _(j):
        here = pl.ds(pl.multiple_of(j * 256, 256), 256)
        tail[0:3, here] = pv[56:PARAMS, here]
        whole = jnp.concatenate([pv[0:56, here], tail[:, here]], axis=0)
        for n, piece in enumerate(split(whole, 3)):
            p3[64 * n : 64 * (n + 1), here] = piece

    picked = dot_nn(p3[...], oh[...])
    gs[...] = picked[0:64] + picked[64:128] + picked[128:192]
    feats = project_rows([gs[f : f + 1, :] for f in range(PARAMS)], [cam[0, k] for k in range(16)])
    fs[8:16, :] = jnp.zeros((8, ROWS), F32)
    for f in range(FEATS):
        fs[f : f + 1, :] = feats[f]

    pl.semaphore_wait(barrier, 18)
    for z in z_near[:2]:
        tell(near_sem, {"gauss": place(mx, z, mc)})
    for y in y_peers:
        tell(view_sem, {"img": y})

    left = iota((8, 128), 1) < 64
    mine = mc * 4 + mx

    def halves(first, second):
        return jnp.where(left, first, pltpu.roll(second, 64, 1)), jnp.where(left, pltpu.roll(first, 64, 1), second)

    def send_z(turn, peers):
        for z in peers:
            pltpu.make_async_remote_copy(
                src_ref=msg.at[turn, :, z], dst_ref=mid.at[turn, :, mz], send_sem=zsend.at[turn], recv_sem=zrecv.at[turn],
                device_id={"gauss": place(mx, z, mc)}, device_id_type=MESH,
            ).start()

    def wait_z(turn, sems):
        span = mid.at[turn, :, pl.ds(0, 15)]
        pltpu.make_async_copy(span, span, sems.at[turn]).wait()

    def send_x(turn, x, c, y, slot):
        pltpu.make_async_remote_copy(
            src_ref=comp.at[turn, c * 4 + x], dst_ref=got.at[slot, mine], send_sem=xsend.at[turn],
            recv_sem=xrecv.at[slot], device_id={"gauss": place(x, mz, c), "img": y}, device_id_type=MESH,
        ).start()

    def wait_x(slot, count):
        span = got.at[slot, pl.ds(0, count)]
        pltpu.make_async_copy(span, span, xrecv.at[slot]).wait()

    def prepare():
        named = jnp.concatenate([lists[0, 0:1, :], lists[0, 1:2, :]], axis=1)
        named = column_of(named)
        names[...] = jnp.broadcast_to(named.astype(F32), (8, ROWS)).T

        @pl.loop(0, 8)
        def _(j):
            start = pl.multiple_of(j * 64, 64)
            ohr[pl.ds(start, 64), :] = where_equal(iota((64, ROWS), 0) + start, named)
            ohs[pl.ds(start, 64), :] = where_equal(iota((64, ROWS), 1).astype(F32), names[pl.ds(start, 64), 0:1])

        earlier = jnp.where(iota((LIST, LIST), 0) < iota((LIST, LIST), 1), 1.0, 0.0).astype(BF16)
        later = jnp.where(iota((LIST, LIST), 0) > iota((LIST, LIST), 1), 1.0, 0.0).astype(BF16)
        for n in range(2):
            upper[LIST * n : LIST * (n + 1), :] = earlier
            lower[LIST * n : LIST * (n + 1), :] = later
        rs[...] = jnp.zeros((2, 16, 256), F32)
        ge[8:16, :] = jnp.zeros((8, ROWS), F32)

    packed = as_message(fs[...])
    for x in range(4):
        comp[0, x], comp[0, 4 + x] = halves(packed[16 * x : 16 * x + 8], packed[16 * x + 8 : 16 * x + 16])
    for x, c in x_others:
        send_x(0, x, c, my, 4)
    got[4, mine] = comp[0, mine]
    for k in range(16):
        info[my, k : k + 1, :] = jnp.zeros((1, 128), F32) + cam[0, k]
    for k in range(4):
        info[my, 16 + k : 17 + k, :] = send_rows[:, k * 128 : (k + 1) * 128].astype(F32)
    info[my, 20:24, :] = jnp.zeros((4, 128), F32)
    for n, y in enumerate(y_peers):
        pltpu.make_async_remote_copy(
            src_ref=info.at[my], dst_ref=info.at[my], send_sem=isend.at[n], recv_sem=irecv.at[n],
            device_id={"img": y}, device_id_type=MESH,
        ).start()
    wait_x(4, 7)
    for x in range(4):
        low_z, high_z = halves(got[4, x], got[4, 4 + x])
        msg.reshape(128, 128)[16 * x : 16 * x + 8, :] = low_z
        msg.reshape(128, 128)[16 * x + 8 : 16 * x + 16, :] = high_z
    send_z(0, z_near)
    pl.semaphore_wait(near_sem, 2)
    send_z(0, z_peers[:7])
    mid[0, :, mz] = msg[0, :, mz]
    prepare()
    wait_z(0, zrecv)
    received = as_columns(mid.reshape(128, 128)[0:64, :])

    listed = dot_nn(jnp.concatenate(split(received, 3), axis=0), ohr[...])
    fe[...] = listed[0:16] + listed[16:32] + listed[32:48]

    def entry(f, t):
        return fe[f : f + 1, t * LIST : (t + 1) * LIST]

    pixel = iota((16, LIST), 0).astype(F32)
    off_x, quad_x, cross, quad_y, origin_y, weight = [], [], [], [], [], []
    for t in range(2):
        tile = tiles[0, t]
        off_x.append(entry(0, t) - (pixel + ((tile & 15) * 16).astype(F32)))
        origin_y.append(entry(1, t) - ((tile >> 4) * 16).astype(F32))
        quad_x.append(-0.5 * entry(2, t) * off_x[t] * off_x[t])
        cross.append(-entry(3, t))
        quad_y.append(-0.5 * entry(4, t))
        weight.append(jnp.where(iota((1, LIST), 1) < counts[0, t], entry(8, t), 0.0))

    def pixels(t, j):
        return pl.ds(pl.multiple_of(t * 256 + j * 16, 16), 16)

    @pl.loop(0, 16, unroll=16)
    def _(j):
        for t in range(2):
            here = pixels(t, j)
            off_y = origin_y[t] - lax.convert_element_type(j, F32)
            power = quad_x[t] + off_x[t] * (cross[t] * off_y) + quad_y[t] * off_y * off_y
            alpha = weight[t] * jnp.exp(power)
            al[here, :] = alpha
            for n, piece in enumerate(split(jnp.log(1.0 - alpha), 2)):
                lk[here, LIST * n : LIST * (n + 1)] = piece

    bf[...] = dot_nn(lk[...], upper[...])

    @pl.loop(0, 16, unroll=16)
    def _(j):
        for t in range(2):
            here = pixels(t, j)
            ws[here, :] = al[here, :] * jnp.exp(bf[here, :])

    grad_colour = []
    for t in range(2):
        shown = split(ws[t * 256 : (t + 1) * 256, :], 3)
        tints = split(fe[:, t * LIST : (t + 1) * LIST], 3)
        stacked = jnp.concatenate(tints, axis=0)
        colours = dot_nt(stacked, shown[0]) + dot_nt(stacked, shown[1]) + dot_nt(stacked, shown[2])
        colours = (colours[0:16] + colours[16:32] + colours[32:48])[5:8]
        rendered[0, :, t, :] = colours
        rs[t, 5:8, :] = colours - targets[0, :, t, :]
        resid = split(rs[t], 2)
        stacked = jnp.concatenate(resid, axis=0)
        tinted = dot_nn(stacked, shown[0]) + dot_nn(stacked, shown[1])
        grad_colour.append(tinted[5:8] + tinted[21:24])
        resid = [piece.astype(F32) for piece in resid]
        turned = jnp.concatenate([resid[0], resid[1], resid[0]], axis=0).T.astype(BF16)
        bf[t * 256 : (t + 1) * 256, :] = dot_nn(turned, jnp.concatenate([tints[0], tints[0], tints[1]], axis=0))

    @pl.loop(0, 16, unroll=16)
    def _(j):
        for t in range(2):
            here = pixels(t, j)
            share = bf[here, :] * ws[here, :]
            ws[here, :] = share
            for n, piece in enumerate(split(share, 2)):
                sw2[here, LIST * n : LIST * (n + 1)] = piece

    bf[...] = dot_nn(sw2[...], lower[...])

    for t in range(2):

        def moments(j, carry):
            here = pixels(t, j)
            alpha = al[here, :]
            off_y = origin_y[t] - lax.convert_element_type(j, F32)
            flow = ws[here, :] - bf[here, :] * (alpha / (1.0 - alpha))
            flow_y = flow * off_y
            return carry[0] + flow, carry[1] + flow_y, carry[2] + flow_y * off_y

        zero = jnp.zeros((16, LIST), F32)
        flow, flow_y, flow_yy = lax.fori_loop(0, 16, moments, (zero, zero, zero), unroll=16)

        def over(value):
            return jnp.sum(value, axis=0, keepdims=True)

        m_x, m_y = over(flow * off_x[t]), over(flow_y)
        a, b, c = entry(2, t), entry(3, t), entry(4, t)
        out = [
            -(a * m_x + b * m_y),
            -(b * m_x + c * m_y),
            -0.5 * over(flow * off_x[t] * off_x[t]),
            -over(flow_y * off_x[t]),
            -0.5 * over(flow_yy),
            grad_colour[t][0:1],
            grad_colour[t][1:2],
            grad_colour[t][2:3],
            over(flow) / entry(8, t),
        ]
        for f in range(FEATS):
            ge[f : f + 1, t * LIST : (t + 1) * LIST] = out[f]

    back = dot_nn(jnp.concatenate(split(ge[...], 2), axis=0), ohs[...])
    msg.reshape(128, 128)[64:128, :] = as_message(back[0:16] + back[16:32])
    pulls = []

    def look_ahead():
        for n in range(3):
            pltpu.make_async_copy(info.at[0], info.at[0], irecv.at[n]).wait()
            pltpu.make_async_copy(info.at[0], info.at[0], isend.at[n]).wait()
        rows = [
            jnp.concatenate([info[view, 16 + k : 17 + k, :] for k in range(4)], axis=1).astype(jnp.int32)
            for view in range(4)
        ]
        for view, picks in enumerate(reorder(rows, True)):
            place_in = (picks - (my * QUARTER).astype(F32)).astype(jnp.int32)
            high[view] = jnp.where(iota((8, ROWS), 0) == (place_in >> 7), 1.0, 0.0)
            low[view] = jnp.where(iota((128, ROWS), 0) == (place_in & 127), 1.0, 0.0).T.astype(BF16)
        for block in range(8):
            pq[block] = pv[:, pl.ds(pl.multiple_of(my * QUARTER + block * 128, 128), 128)]
        own = [pq[:, f, :] for f in range(PARAMS)]
        for view in [my] + y_peers:
            camera = [jnp.broadcast_to(info[view, k : k + 1, :], (8, 128)) for k in range(16)]
            pulls.append(jax.vjp(lambda rows, camera=camera: project_rows(rows, camera), own)[1])

    send_z(1, z_peers)
    mid[1, :, mz] = msg[1, :, mz]
    look_ahead()
    wait_z(1, zrecv)
    for x in range(4):
        whole = mid.reshape(128, 128)[64 + 16 * x : 80 + 16 * x, :]
        comp[1, x], comp[1, 4 + x] = halves(whole[0:8], whole[8:16])
    pl.semaphore_wait(view_sem, 3)
    steps = [(x, c, y) for x in range(4) for c in range(2) for y in range(4) if (x, c, y) != (0, 0, 0)]
    steps.sort(key=lambda step: -min(step[0], 4 - step[0]) - min(step[2], 4 - step[2]))
    for x, c, y in steps:
        send_x(1, (mx + x) % 4, (mc + c) % 2, (my + y) % 4, my)
    got[my, mine] = comp[1, mine]
    for turn in range(2):
        wait_z(turn, zsend)

    def pulled(view, number):
        cols = as_columns(got[view].reshape(64, 128))
        parts = [high[view] * cols[f : f + 1] for f in range(FEATS)] + [jnp.zeros((8, ROWS), F32)]
        parts = split(jnp.concatenate(parts, axis=0), 2)
        sums = dot_nn(jnp.concatenate(parts, axis=0), low[view])
        sums = sums[0:80] + sums[80:160]
        (out,) = pulls[number]([sums[8 * f : 8 * f + 8] for f in range(FEATS)])
        return out

    wait_x(my, 7)
    total = pulled(my, 0)
    for y in y_peers:
        wait_x(y, 8)
    for n, y in ((1, y_peers[1]), (2, y_peers[2]), (0, y_peers[0])):
        total = [a + b for a, b in zip(total, pulled(y, n + 1))]
    for f in range(PARAMS):
        gq[:, f, :] = total[f]
    span = comp.at[0, pl.ds(0, 7)]
    pltpu.make_async_copy(span, span, xsend.at[0]).wait()
    span = got.at[0, pl.ds(0, 7)]
    pltpu.make_async_copy(span, span, xsend.at[1]).wait()
    span = got.at[pl.ds(0, 3)]
    pltpu.make_async_copy(span, span, xsend.at[1]).wait()


def finish(blocks, shown, grads, rendered, sem):
    copies = [pltpu.make_async_copy(blocks.at[b], grads.at[:, pl.ds(b * 128, 128)], sem.at[b]) for b in range(8)]
    copies.append(pltpu.make_async_copy(shown, rendered, sem.at[8]))
    for copy in copies:
        copy.start()
    for copy in copies:
        copy.wait()


def local(params, cameras, send_rows, tile_ids, lists, counts, targets):
    vmem, anywhere = (pl.BlockSpec(memory_space=s) for s in (pltpu.VMEM, pl.ANY))
    dma = pltpu.SemaphoreType.DMA
    operands = (params, cameras, send_rows, tile_ids, lists, counts, jnp.transpose(targets, (0, 2, 1, 3)))
    blocks, shown = pl.pallas_call(
        kernel,
        out_shape=(
            pltpu.VMEM((8, PARAMS, 128), F32),
            pltpu.VMEM((1, 3, 2, 256), F32),
        ),
        in_specs=[anywhere] * 7,
        out_specs=(vmem, vmem),
        scratch_shapes=[
            pltpu.SMEM((1, 16), F32),
            pltpu.VMEM((1, ROWS), jnp.int32),
            pltpu.SMEM((1, 2), jnp.int32),
            pltpu.VMEM((1, 2, LIST), jnp.int32),
            pltpu.SMEM((1, 2), jnp.int32),
            pltpu.VMEM((1, 3, 2, 256), F32),
            dma((6,)),
            pltpu.VMEM((PARAMS, G_DEV), F32),
            pltpu.VMEM((8, G_DEV), F32),
            pltpu.VMEM((8, PARAMS, 128), F32),
            pltpu.VMEM((4, 24, 128), F32),
            pltpu.VMEM((192, G_DEV), BF16),
            pltpu.VMEM((G_DEV, ROWS), BF16),
            pltpu.VMEM((4, 8, ROWS), F32),
            pltpu.VMEM((4, ROWS, 128), BF16),
            pltpu.VMEM((64, ROWS), F32),
            pltpu.VMEM((16, ROWS), F32),
            pltpu.VMEM((2, 4, 16, 1, 128), F32),
            pltpu.VMEM((2, 4, 16, 1, 128), F32),
            pltpu.VMEM((2, 8, 8, 128), F32),
            pltpu.VMEM((5, 8, 8, 128), F32),
            pltpu.VMEM((ROWS, ROWS), BF16),
            pltpu.VMEM((ROWS, ROWS), BF16),
            pltpu.VMEM((ROWS, 8), F32),
            pltpu.VMEM((2 * LIST, LIST), BF16),
            pltpu.VMEM((2 * LIST, LIST), BF16),
            pltpu.VMEM((16, ROWS), F32),
            pltpu.VMEM((512, LIST), F32),
            pltpu.VMEM((512, 2 * LIST), BF16),
            pltpu.VMEM((512, LIST), F32),
            pltpu.VMEM((512, LIST), F32),
            pltpu.VMEM((512, 2 * LIST), BF16),
            pltpu.VMEM((2, 16, 256), F32),
            pltpu.VMEM((16, ROWS), F32),
            dma,
            dma((3,)),
            dma((3,)),
            dma((2,)),
            dma((2,)),
            dma((2,)),
            dma((5,)),
            pltpu.SemaphoreType.REGULAR,
            pltpu.SemaphoreType.REGULAR,
        ],
        compiler_params=pltpu.CompilerParams(
            collective_id=0, has_side_effects=True, vmem_limit_bytes=32 * 1024 * 1024
        ),
    )(*(pltpu.with_memory_space_constraint(operand, pltpu.HBM) for operand in operands))
    grads, shown = pl.pallas_call(
        finish,
        out_shape=(
            jax.ShapeDtypeStruct((PARAMS, QUARTER), F32),
            jax.ShapeDtypeStruct((1, 3, 2, 256), F32),
        ),
        in_specs=[anywhere, anywhere],
        out_specs=(anywhere, anywhere),
        scratch_shapes=[dma((9,))],
    )(*(pltpu.with_memory_space_constraint(part, pltpu.VMEM) for part in (blocks, shown)))
    return grads, jnp.transpose(shown, (0, 2, 1, 3))


def solution(mesh):
    placed = (
        P(None, "gauss"),
        P("img", None),
        P("img", "gauss"),
        P("img", "gauss"),
        P("img", "gauss", None),
        P("img", "gauss"),
        P("img", "gauss", None, None),
    )
    return jax.shard_map(
        local,
        mesh=mesh,
        in_specs=placed,
        out_specs=(P(None, ("gauss", "img")), P("img", "gauss", None, None)),
        check_vma=False,
    )
```
